32 devices in a mesh: band: 2 (over x), spk: 16 (over z, y, core).
Axes of the slice: x: 2, y: 2, z: 4, core: 2. Of those that a mesh axis runs over, the one named last changes fastest.
Arguments:
- direction: float32 [64, 128, 128], P(('band', 'spk')), parts along dimension 0, may hold values from -6 to 6
- plant: bfloat16 [832, 2, 128, 128], P(('band', 'spk')), parts along dimension 0
- tile_pairs: int32 [832, 2], P(('band', 'spk')), parts along dimension 0, may hold values from 0 to 127, as said below
- mic_weight: float32 [2, 128, 128], P('band', 'spk'), parts along dimension 0, may hold values from 0.3 to 3
Outputs:
- hessian_vector: float32 [64, 128, 128], P(('band', 'spk')), parts along dimension 0
The draws below stay inside these ranges and needn't reach their ends.
There are 2 independent parts, one for each index of `band`. The reference program is written for one: setup_inputs(seed, part) draws one part's arguments, and reference() takes and returns one part's arrays. A program takes and returns all parts, laid end to end along the dimension named above; each array names one. Nothing has to cross between parts.
Inputs may be any that keep to these rules, and one draw needn't show every extreme that they name: `tile_pairs`: column 0 is a speaker block, column 1 a microphone block. The rows of one device (aligned blocks of 26 rows) all lie in that device's bin, and their speaker blocks s satisfy s // 2 = (device index) % 16; no pair repeats on a device. Counting microphone blocks m by the device m * 16 // 128, at most 4 rows of one device fall to any one device, and in every part one device gets exactly 4 from every device.
All inputs are finite; a program needn't handle non-finite values.
Results may differ from the reference program's by a relative error of at most 0.0032.
Values may be sent and summed in bfloat16 or wider, within the bound.
A program may use at most 128 MiB of HBM per device.

```python
import math
import jax
import jax.numpy as jnp
from jax import lax

BLK = 128
SBLK = 32
MBLK = 128
R = 64
UNIT_DEV = 2
SPEAKERS = 4096
BINS = 1
UNITS = 32
TILE_DEV = 26
TILES = 416
MOST = 4


def draw_plant(key, part):
    keys = jax.random.split(jax.random.fold_in(key, 11), 4)
    shape = (TILES, 2, BLK, BLK)
    base = jax.random.normal(keys[0], shape, jnp.float32)
    row_scale = jnp.power(10.0, jax.random.uniform(keys[1], (TILES, 1, BLK, 1), jnp.float32) - 0.5)
    col_scale = jnp.power(10.0, jax.random.uniform(keys[2], (TILES, 1, 1, BLK), jnp.float32) - 0.5)
    tile_scale = jnp.power(10.0, jax.random.uniform(keys[3], (TILES, 1, 1, 1), jnp.float32) - 0.5)
    values = base * row_scale * col_scale * tile_scale * (0.1 / BLK ** 0.5)
    return values.astype(jnp.bfloat16)


def draw_tile_pairs(key, part):
    devices = TILES // TILE_DEV
    slot_count = devices * MOST
    peer_blocks = MBLK // devices
    combos = UNIT_DEV * peer_blocks
    groups = SBLK // UNIT_DEV
    full_peer = jax.random.randint(jax.random.fold_in(key, 7), (), 0, devices)

    def one_device(device):
        dev_key = jax.random.fold_in(key, device + 100)
        first_key, second_key, third_key = jax.random.split(dev_key, 3)
        ranking = jax.random.permutation(first_key, slot_count)
        slot_peer = jnp.arange(slot_count) // MOST
        scores = jnp.where(slot_peer == full_peer, ranking - slot_count, ranking)
        chosen = jnp.argsort(scores, stable=True)[:TILE_DEV]
        chosen = chosen[jax.random.permutation(second_key, TILE_DEV)]

        def peer_combos(peer_key):
            return jax.random.permutation(peer_key, combos)[:MOST]
        combo_table = jax.vmap(peer_combos)(jax.random.split(third_key, devices))
        chosen_peer = chosen // MOST
        chosen_slot = chosen % MOST
        combo = combo_table[chosen_peer, chosen_slot]
        unit_local = combo // peer_blocks
        mic_block = chosen_peer * peer_blocks + combo % peer_blocks
        speaker_block = device % groups * UNIT_DEV + unit_local
        return jnp.stack([speaker_block, mic_block], axis=1)
    result = jax.vmap(one_device)(jnp.arange(devices))
    return result.reshape(TILES, 2).astype(jnp.int32)


def level_of(key, dims, pieces, least, largest):
    factor_of, own = 1.0, jax.random.fold_in(key, 6)
    for position, parts in pieces:
        heights = jnp.exp(jax.random.uniform(jax.random.fold_in(own, position), (parts,), jnp.float32, least / len(pieces), largest / len(pieces)))
        factor_of = factor_of * jnp.repeat(heights, dims[position] // parts).reshape([-1 if axis == position else 1 for axis in range(len(dims))])
    return factor_of


def scatter_about(stream_key, extent, width, bound, cuts=(), kind=jnp.bfloat16):
    loudness = level_of(stream_key, extent, cuts, -0.22, 0.18) if cuts else 1.0
    drawn = jax.random.normal(stream_key, extent, jnp.float32) * width * loudness
    return jnp.minimum(jnp.maximum(drawn, -bound), bound).astype(kind)


def setup_inputs(seed: int = 0, part: int = 0) -> dict:
    streams_of = jax.random.split(jax.random.key(seed), 5)
    own_keys = jax.random.split(jax.random.fold_in(streams_of[4], part), 5)
    return {
        "direction": scatter_about(own_keys[0], (UNITS, BLK, 2 * R), 1.0, 6.0, ((0, 16),), jnp.float32),
        "plant": draw_plant(jax.random.fold_in(jax.random.fold_in(streams_of[4], part), 71), part),
        "tile_pairs": draw_tile_pairs(jax.random.fold_in(jax.random.fold_in(streams_of[4], part), 71), part),
        "mic_weight": jnp.clip(jnp.exp(math.log(3.0) - 2.3025851 * jax.random.uniform(own_keys[3], (BINS, MBLK, BLK), jnp.float32) ** level_of(own_keys[3], (BINS, MBLK, BLK), ((1, 16),), -0.2, 0.2)), 0.3, 3.0),
    }


reg_weight = 0.25


def reference(direction, plant, tile_pairs, mic_weight):
    highest = lax.Precision.HIGHEST
    tile_index = jnp.arange(TILES, dtype=jnp.int32)
    tile_bin = ((tile_index // TILE_DEV) * UNIT_DEV // SBLK).astype(jnp.int32)
    speaker_unit = (tile_bin * SBLK + tile_pairs[:, 0]).astype(jnp.int32)
    mic_unit = (tile_bin * MBLK + tile_pairs[:, 1]).astype(jnp.int32)
    rounded = lax.optimization_barrier(direction.astype(jnp.bfloat16)).astype(jnp.float32)
    plant_wide = plant.astype(jnp.float32)
    forward = jnp.einsum('tcij,tjk->tcik', plant_wide, rounded[speaker_unit], precision=highest)
    partial_field = jnp.concatenate([forward[:, 0, :, :R] - forward[:, 1, :, R:], forward[:, 0, :, R:] + forward[:, 1, :, :R]], axis=-1)
    pressure = jax.ops.segment_sum(partial_field, mic_unit, num_segments=BINS * MBLK)
    weights_flat = mic_weight.reshape(BINS * MBLK, BLK)
    weighted = lax.optimization_barrier((weights_flat[:, :, None] * pressure).astype(jnp.bfloat16)).astype(jnp.float32)
    adjoint = jnp.einsum('tcij,tik->tcjk', plant_wide, weighted[mic_unit], precision=highest)
    back_field = jnp.concatenate([adjoint[:, 0, :, :R] + adjoint[:, 1, :, R:], adjoint[:, 0, :, R:] - adjoint[:, 1, :, :R]], axis=-1)
    gram = jax.ops.segment_sum(back_field, speaker_unit, num_segments=UNITS)
    tile_power = jnp.sum(jnp.square(plant_wide), axis=(1, 2, 3))
    bin_power = jax.ops.segment_sum(tile_power, tile_bin, num_segments=BINS)
    unit_power = jnp.repeat(bin_power, SBLK)
    return gram + reg_weight * unit_power[:, None, None] / SPEAKERS * direction
```

```python
import functools

import jax
import jax.numpy as jnp
from jax import lax
from jax.experimental import pallas as pl
from jax.experimental.pallas import tpu as pltpu
from jax.sharding import PartitionSpec as P

SBLK = 32
MBLK = 128
SPEAKERS = 4096
CHUNK = 2

reg_weight = 0.25

MESH = pl.DeviceIdType.MESH


def kernel(
    group, fwd_idx, back_idx, direction, plant, weights, out,
    info, packed, flipped, fields, sib_out, sib_in, own, y_out, y_in,
    right_out, left_out, from_left, from_right, weighted, stacked,
    info_s, info_r, sib_s, sib_r, y_s, y_r, right_s, right_r, left_s, left_r,
    ws_s, ws_r, wy_s, wy_r, wf_s, wf_r,
):
    units, block, width = direction.shape
    tiles = plant.shape[0]
    quarter = MBLK // 4
    chunks = quarter // CHUNK
    rows_per = MBLK // group
    depth = group // 4
    half = width // 2

    me = lax.axis_index("spk")
    base = (me // group) * group
    rank = me - base
    z = rank // 4
    y = (rank // 2) % 2
    c = rank % 2
    sib = me + 1 - 2 * c
    other_y = me + 2 - 4 * y
    q_mine = y * 2 + c
    q_sib = y * 2 + 1 - c
    q_y = (1 - y) * 2 + c
    q_diag = (1 - y) * 2 + 1 - c
    has_left = z > 0
    has_right = z < depth - 1

    def peer(j):
        return base + (rank + j) % group

    def copy(src, dst, send, recv, device):
        return pltpu.make_async_remote_copy(
            src_ref=src, dst_ref=dst, send_sem=send, recv_sem=recv,
            device_id={"spk": device}, device_id_type=MESH,
        )

    barrier = pltpu.get_barrier_semaphore()
    for j in range(1, group):
        pl.semaphore_signal(barrier, inc=1, device_id={"spk": peer(j)}, device_id_type=MESH)

    lane = lax.broadcasted_iota(jnp.int32, (block, width), 1)
    for u in range(units):
        x = direction[u]
        turned = pltpu.roll(x, half, 1)
        turned = jnp.where(lane < half, -turned, turned)
        fields[u, :block, :] = x.astype(jnp.bfloat16)
        fields[u, block:, :] = turned.astype(jnp.bfloat16)

    def pack(t, power):
        p0 = plant[t, 0]
        p1 = plant[t, 1]
        packed[t, :, :block] = p0
        packed[t, :, block:] = p1
        f0 = p0.astype(jnp.float32)
        f1 = p1.astype(jnp.float32)
        squares = f0 * f0 + f1 * f1
        return power + jnp.sum(squares.reshape(block // 8, 8, block), axis=0)

    power = lax.fori_loop(0, tiles, pack, jnp.zeros((8, block), jnp.float32))
    packed[tiles] = jnp.zeros((block, 2 * block), jnp.bfloat16)
    weighted[MBLK] = jnp.zeros((block, width), jnp.bfloat16)
    info[rank, :rows_per, :] = weights[...]
    info[rank, rows_per:, :] = power

    pl.semaphore_wait(barrier, group - 1)

    def info_copy(j):
        return copy(info.at[rank], info.at[rank], info_s.at[j], info_r.at[j], peer(j))

    def sib_copy(k):
        return copy(sib_out.at[k], sib_in.at[k], sib_s.at[k], sib_r.at[k], sib)

    def y_copy(k):
        return copy(y_out.at[k], y_in.at[k], y_s.at[k], y_r.at[k], other_y)

    def right_copy(k):
        return copy(right_out.at[k], from_left.at[k], right_s.at[k], right_r.at[k], me + 4)

    def left_copy(k):
        return copy(left_out.at[k], from_right.at[k], left_s.at[k], left_r.at[k], me - 4)

    def part(q, k):
        return weighted.at[pl.ds(q * quarter + k * CHUNK, CHUNK)]

    def ws_copy(k):
        return copy(part(q_mine, k), part(q_mine, k), ws_s.at[k], ws_r.at[k], sib)

    def wy_copy(k):
        return copy(part(q_mine, k), part(q_mine, k), wy_s.at[k], wy_r.at[k], other_y)

    def wf_copy(k):
        return copy(part(q_y, k), part(q_y, k), wf_s.at[k], wf_r.at[k], sib)

    for j in range(1, group):
        info_copy(j).start()

    def product(v):
        total = jnp.dot(packed[fwd_idx[v * units]], fields[0], preferred_element_type=jnp.float32)
        for u in range(1, units):
            total += jnp.dot(
                packed[fwd_idx[v * units + u]], fields[u], preferred_element_type=jnp.float32
            )
        return total

    def inside(k):
        return jnp.logical_and(k >= 0, k < chunks)

    def step(s, carry):
        @pl.when(inside(s))
        def _():
            k = s
            for i in range(CHUNK):
                at = k * CHUNK + i
                sib_out[k, i] = product(q_sib * quarter + at).astype(jnp.bfloat16)
                sib_out[k, CHUNK + i] = product(q_diag * quarter + at).astype(jnp.bfloat16)
            sib_copy(k).start()
            for i in range(CHUNK):
                at = k * CHUNK + i
                own[k, i] = product(q_mine * quarter + at)
                own[k, CHUNK + i] = product(q_y * quarter + at)

        k1 = s - 1

        @pl.when(inside(k1))
        def _():
            sib_copy(k1).wait_recv()
            for i in range(CHUNK):
                total = own[k1, CHUNK + i] + sib_in[k1, CHUNK + i].astype(jnp.float32)
                y_out[k1, i] = total.astype(jnp.bfloat16)
            y_copy(k1).start()
            for i in range(CHUNK):
                own[k1, i] = own[k1, i] + sib_in[k1, i].astype(jnp.float32)

        k2 = s - 2

        @pl.when(inside(k2))
        def _():
            y_copy(k2).wait_recv()
            for i in range(CHUNK):
                own[k2, i] = own[k2, i] + y_in[k2, i].astype(jnp.float32)

        kr = s - 2 - z

        @pl.when(inside(kr))
        def _():
            @pl.when(has_left)
            def _():
                right_copy(kr).wait_recv()

            @pl.when(jnp.logical_and(has_left, has_right))
            def _():
                for i in range(CHUNK):
                    total = own[kr, i] + from_left[kr, i].astype(jnp.float32)
                    right_out[kr, i] = total.astype(jnp.bfloat16)

            @pl.when(jnp.logical_not(has_left))
            def _():
                for i in range(CHUNK):
                    right_out[kr, i] = own[kr, i].astype(jnp.bfloat16)

            @pl.when(has_right)
            def _():
                right_copy(kr).start()

        kl = s - 2 - (depth - 1 - z)

        @pl.when(inside(kl))
        def _():
            @pl.when(has_right)
            def _():
                left_copy(kl).wait_recv()

            @pl.when(jnp.logical_and(has_left, has_right))
            def _():
                for i in range(CHUNK):
                    total = own[kl, i] + from_right[kl, i].astype(jnp.float32)
                    left_out[kl, i] = total.astype(jnp.bfloat16)

            @pl.when(jnp.logical_not(has_right))
            def _():
                for i in range(CHUNK):
                    left_out[kl, i] = own[kl, i].astype(jnp.bfloat16)

            @pl.when(has_left)
            def _():
                left_copy(kl).start()

        kt = s - 2 - jnp.maximum(z, depth - 1 - z)

        @pl.when(kt == 0)
        def _():
            for j in range(1, group):
                info_copy(j).wait_recv()

        @pl.when(inside(kt))
        def _():
            @pl.when(has_left)
            def _():
                for i in range(CHUNK):
                    own[kt, i] = own[kt, i] + from_left[kt, i].astype(jnp.float32)

            @pl.when(has_right)
            def _():
                for i in range(CHUNK):
                    own[kt, i] = own[kt, i] + from_right[kt, i].astype(jnp.float32)

            for i in range(CHUNK):
                v = q_mine * quarter + kt * CHUNK + i
                row = info[v // rows_per, pl.ds(v % rows_per, 1), :]
                scale = jnp.broadcast_to(row, (block, block)).T
                weighted[v] = (scale * own[kt, i]).astype(jnp.bfloat16)
            wy_copy(kt).start()
            ws_copy(kt).start()

        kd = kt - 1

        @pl.when(inside(kd))
        def _():
            wy_copy(kd).wait_recv()
            wf_copy(kd).start()

        for n in range(2):
            t = s * 2 + n

            @pl.when(t < tiles)
            def _():
                flipped[t, :block, :] = plant[t, 0].T
                flipped[t, block:, :] = plant[t, 1].T

        return carry

    steps = max(chunks + 3 + depth - 1, (tiles + 1) // 2)
    lax.fori_loop(0, steps, step, 0)

    def arrived(k, carry):
        ws_copy(k).wait_recv()
        wf_copy(k).wait_recv()
        return carry

    lax.fori_loop(0, chunks, arrived, 0)

    for t in range(tiles):
        for u in range(units):
            stacked[t, :, u * width:(u + 1) * width] = weighted[back_idx[t * units + u]]
    total = jnp.zeros((2 * block, units * width), jnp.float32)
    for t in range(tiles):
        total += jnp.dot(flipped[t], stacked[t], preferred_element_type=jnp.float32)

    power_sum = jnp.sum(info[:, rows_per:, :], axis=0)
    power_sum = jnp.sum(jnp.sum(power_sum, axis=1, keepdims=True), axis=0, keepdims=True)
    coefficient = reg_weight * power_sum / SPEAKERS
    for u in range(units):
        straight = total[:block, u * width:(u + 1) * width]
        crossed = pltpu.roll(total[block:, u * width:(u + 1) * width], half, 1)
        crossed = jnp.where(lane < half, crossed, -crossed)
        out[u] = straight + crossed + coefficient * direction[u]

    for j in range(1, group):
        info_copy(j).wait_send()

    def sent(k, carry):
        sib_copy(k).wait_send()
        y_copy(k).wait_send()
        ws_copy(k).wait_send()
        wy_copy(k).wait_send()
        wf_copy(k).wait_send()

        @pl.when(has_right)
        def _():
            right_copy(k).wait_send()

        @pl.when(has_left)
        def _():
            left_copy(k).wait_send()

        return carry

    lax.fori_loop(0, chunks, sent, 0)


def per_device(direction, plant, tile_pairs, mic_weight):
    device_id = lax.axis_index("spk")
    units, block, width = direction.shape
    tiles = plant.shape[0]
    bins = mic_weight.shape[0]
    group = SBLK // units
    quarter = MBLK // 4
    chunks = quarter // CHUNK
    rows_per = MBLK // group

    if bins == 1:
        weights = mic_weight.reshape(rows_per, block)
    else:
        whole = lax.all_gather(mic_weight, "spk", axis=1, tiled=True)
        weights = lax.dynamic_slice(
            whole, (device_id // group, (device_id % group) * rows_per, 0), (1, rows_per, block)
        )[0]

    unit = tile_pairs[:, 0] % units
    mic = tile_pairs[:, 1]
    unit_hit = unit[:, None] == jnp.arange(units, dtype=jnp.int32)[None, :]
    mic_hit = mic[:, None] == jnp.arange(MBLK, dtype=jnp.int32)[None, :]
    both = jnp.logical_and(mic_hit[:, :, None], unit_hit[:, None, :])
    order = tiles - jnp.arange(tiles, dtype=jnp.int32)
    fwd_idx = tiles - jnp.sum(jnp.where(both, order[:, None, None], 0), axis=0)
    back_idx = jnp.where(unit_hit, mic[:, None], MBLK)

    bf16, f32 = jnp.bfloat16, jnp.float32
    dma = pltpu.SemaphoreType.DMA
    vmem = pl.BlockSpec(memory_space=pltpu.VMEM)
    smem = pl.BlockSpec(memory_space=pltpu.SMEM)
    piece = (chunks, CHUNK, block, width)
    double = (chunks, 2 * CHUNK, block, width)
    return pl.pallas_call(
        functools.partial(kernel, group),
        out_shape=jax.ShapeDtypeStruct(direction.shape, f32),
        in_specs=[smem, smem, vmem, vmem, vmem],
        out_specs=vmem,
        scratch_shapes=[
            pltpu.VMEM((group, rows_per + 8, block), f32),
            pltpu.VMEM((tiles + 1, block, 2 * block), bf16),
            pltpu.VMEM((tiles, 2 * block, block), bf16),
            pltpu.VMEM((units, 2 * block, width), bf16),
            pltpu.VMEM(double, bf16),
            pltpu.VMEM(double, bf16),
            pltpu.VMEM(double, f32),
            pltpu.VMEM(piece, bf16),
            pltpu.VMEM(piece, bf16),
            pltpu.VMEM(piece, bf16),
            pltpu.VMEM(piece, bf16),
            pltpu.VMEM(piece, bf16),
            pltpu.VMEM(piece, bf16),
            pltpu.VMEM((MBLK + 1, block, width), bf16),
            pltpu.VMEM((tiles, block, units * width), bf16),
            dma((group,)), dma((group,)),
        ] + [dma((chunks,)) for _ in range(14)],
        compiler_params=pltpu.CompilerParams(
            collective_id=0, has_side_effects=True, vmem_limit_bytes=48 * 1024 * 1024
        ),
        name="pressure_matching",
    )(fwd_idx.reshape(-1), back_idx.reshape(-1), direction, plant, weights)


def solution(mesh):
    placed = (
        P(("band", "spk"), None, None),
        P(("band", "spk"), None, None, None),
        P(("band", "spk"), None),
        P("band", "spk", None),
    )
    return jax.shard_map(
        per_device,
        mesh=mesh,
        in_specs=placed,
        out_specs=P(("band", "spk"), None, None),
        check_vma=False,
    )
```

```python
import functools

import jax
import jax.numpy as jnp
from jax import lax
from jax.experimental import pallas as pl
from jax.experimental.pallas import tpu as pltpu
from jax.sharding import PartitionSpec as P

SBLK = 32
MBLK = 128
SPEAKERS = 4096
CHUNK = 2

reg_weight = 0.25

MESH = pl.DeviceIdType.MESH


def kernel(
    group, fwd_idx, pair_key, direction_in, plant_in, weights_in, out,
    direction, plant, weights, info, products, flipped, fields, sib_out, sib_in, own, y_out, y_in,
    right_out, left_out, from_left, from_right, weighted, stacked,
    load_s, info_s, info_r, sib_s, sib_r, y_s, y_r, right_s, right_r, left_s, left_r,
    ws_s, ws_r, wy_s, wy_r, wf_s, wf_r,
):
    units, block, width = direction.shape
    tiles = plant.shape[0]
    quarter = MBLK // 4
    chunks = quarter // CHUNK
    rows_per = MBLK // group
    depth = group // 4
    half = width // 2

    me = lax.axis_index("spk")
    base = (me // group) * group
    rank = me - base
    z = rank // 4
    y = (rank // 2) % 2
    c = rank % 2
    sib = me + 1 - 2 * c
    other_y = me + 2 - 4 * y
    q_mine = y * 2 + c
    q_sib = y * 2 + 1 - c
    q_y = (1 - y) * 2 + c
    q_diag = (1 - y) * 2 + 1 - c
    has_left = z > 0
    has_right = z < depth - 1

    def peer(j):
        return base + (rank + j) % group

    def copy(src, dst, send, recv, device):
        return pltpu.make_async_remote_copy(
            src_ref=src, dst_ref=dst, send_sem=send, recv_sem=recv,
            device_id={"spk": device}, device_id_type=MESH,
        )

    loads = [
        pltpu.make_async_copy(src, dst, load_s.at[n])
        for n, (src, dst) in enumerate(
            [(direction_in, direction), (plant_in, plant), (weights_in, weights)]
        )
    ]
    for load in loads:
        load.start()
    barrier = pltpu.get_barrier_semaphore()
    for j in range(1, group):
        pl.semaphore_signal(barrier, inc=1, device_id={"spk": peer(j)}, device_id_type=MESH)

    loads[0].wait()
    lane = lax.broadcasted_iota(jnp.int32, (block, width), 1)
    for u in range(units):
        x = direction[u]
        turned = pltpu.roll(x, half, 1)
        turned = jnp.where(lane < half, -turned, turned)
        fields[:block, u * width:(u + 1) * width] = x.astype(jnp.bfloat16)
        fields[block:, u * width:(u + 1) * width] = turned.astype(jnp.bfloat16)
    loads[1].wait()

    def pack(t, power):
        p0 = plant[t, 0]
        p1 = plant[t, 1]
        both = jnp.dot(
            jnp.concatenate([p0, p1], axis=1), fields[...], preferred_element_type=jnp.float32
        )
        for u in range(units):
            products[t * units + u] = both[:, u * width:(u + 1) * width]
        f0 = p0.astype(jnp.float32)
        f1 = p1.astype(jnp.float32)
        squares = f0 * f0 + f1 * f1
        return power + jnp.sum(squares.reshape(block // 8, 8, block), axis=0)

    power = lax.fori_loop(0, tiles, pack, jnp.zeros((8, block), jnp.float32))
    products[tiles * units] = jnp.zeros((block, width), jnp.float32)
    weighted[MBLK] = jnp.zeros((block, width), jnp.bfloat16)
    loads[2].wait()
    info[rank, :rows_per, :] = weights[...]
    info[rank, rows_per:, :] = power

    pl.semaphore_wait(barrier, group - 1)

    def info_copy(j):
        return copy(info.at[rank], info.at[rank], info_s.at[j], info_r.at[j], peer(j))

    def sib_copy(k):
        return copy(sib_out.at[k], sib_in.at[k], sib_s.at[k], sib_r.at[k], sib)

    def y_copy(k):
        return copy(y_out.at[k], y_in.at[k], y_s.at[k], y_r.at[k], other_y)

    def right_copy(k):
        return copy(right_out.at[k], from_left.at[k], right_s.at[k], right_r.at[k], me + 4)

    def left_copy(k):
        return copy(left_out.at[k], from_right.at[k], left_s.at[k], left_r.at[k], me - 4)

    def part(q, k):
        return weighted.at[pl.ds(q * quarter + k * CHUNK, CHUNK)]

    def ws_copy(k):
        return copy(part(q_mine, k), part(q_mine, k), ws_s.at[k], ws_r.at[k], sib)

    def wy_copy(k):
        return copy(part(q_mine, k), part(q_mine, k), wy_s.at[k], wy_r.at[k], other_y)

    def wf_copy(k):
        return copy(part(q_y, k), part(q_y, k), wf_s.at[k], wf_r.at[k], sib)

    for j in range(1, group):
        info_copy(j).start()

    def product(v):
        total = products[fwd_idx[v * units]]
        for u in range(1, units):
            total += products[fwd_idx[v * units + u]]
        return total

    def inside(k):
        return jnp.logical_and(k >= 0, k < chunks)

    def step(s, carry):
        @pl.when(inside(s))
        def _():
            k = s
            for i in range(CHUNK):
                at = k * CHUNK + i
                sib_out[k, i] = product(q_sib * quarter + at).astype(jnp.bfloat16)
                sib_out[k, CHUNK + i] = product(q_diag * quarter + at).astype(jnp.bfloat16)
            sib_copy(k).start()
            for i in range(CHUNK):
                at = k * CHUNK + i
                own[k, i] = product(q_mine * quarter + at)
                own[k, CHUNK + i] = product(q_y * quarter + at)

        k1 = s - 1

        @pl.when(inside(k1))
        def _():
            sib_copy(k1).wait_recv()
            for i in range(CHUNK):
                total = own[k1, CHUNK + i] + sib_in[k1, CHUNK + i].astype(jnp.float32)
                y_out[k1, i] = total.astype(jnp.bfloat16)
            y_copy(k1).start()
            for i in range(CHUNK):
                own[k1, i] = own[k1, i] + sib_in[k1, i].astype(jnp.float32)

        k2 = s - 2

        @pl.when(inside(k2))
        def _():
            y_copy(k2).wait_recv()
            for i in range(CHUNK):
                own[k2, i] = own[k2, i] + y_in[k2, i].astype(jnp.float32)

        kr = s - 2 - z

        @pl.when(inside(kr))
        def _():
            @pl.when(has_left)
            def _():
                right_copy(kr).wait_recv()

            @pl.when(jnp.logical_and(has_left, has_right))
            def _():
                for i in range(CHUNK):
                    total = own[kr, i] + from_left[kr, i].astype(jnp.float32)
                    right_out[kr, i] = total.astype(jnp.bfloat16)

            @pl.when(jnp.logical_not(has_left))
            def _():
                for i in range(CHUNK):
                    right_out[kr, i] = own[kr, i].astype(jnp.bfloat16)

            @pl.when(has_right)
            def _():
                right_copy(kr).start()

        kl = s - 2 - (depth - 1 - z)

        @pl.when(inside(kl))
        def _():
            @pl.when(has_right)
            def _():
                left_copy(kl).wait_recv()

            @pl.when(jnp.logical_and(has_left, has_right))
            def _():
                for i in range(CHUNK):
                    total = own[kl, i] + from_right[kl, i].astype(jnp.float32)
                    left_out[kl, i] = total.astype(jnp.bfloat16)

            @pl.when(jnp.logical_not(has_right))
            def _():
                for i in range(CHUNK):
                    left_out[kl, i] = own[kl, i].astype(jnp.bfloat16)

            @pl.when(has_left)
            def _():
                left_copy(kl).start()

        kt = s - 2 - jnp.maximum(z, depth - 1 - z)

        @pl.when(kt == 0)
        def _():
            for j in range(1, group):
                info_copy(j).wait_recv()

        @pl.when(inside(kt))
        def _():
            @pl.when(has_left)
            def _():
                for i in range(CHUNK):
                    own[kt, i] = own[kt, i] + from_left[kt, i].astype(jnp.float32)

            @pl.when(has_right)
            def _():
                for i in range(CHUNK):
                    own[kt, i] = own[kt, i] + from_right[kt, i].astype(jnp.float32)

            for i in range(CHUNK):
                v = q_mine * quarter + kt * CHUNK + i
                row = info[v // rows_per, pl.ds(v % rows_per, 1), :]
                scale = jnp.broadcast_to(row, (block, block)).T
                weighted[v] = (scale * own[kt, i]).astype(jnp.bfloat16)
            wy_copy(kt).start()
            ws_copy(kt).start()

        kd = kt - 1

        @pl.when(inside(kd))
        def _():
            wy_copy(kd).wait_recv()
            wf_copy(kd).start()

        for n in range(2):
            t = s * 2 + n

            @pl.when(t < tiles)
            def _():
                flipped[t, :block, :] = plant[t, 0].T
                flipped[t, block:, :] = plant[t, 1].T

        return carry

    steps = max(chunks + 3 + depth - 1, (tiles + 1) // 2)
    lax.fori_loop(0, steps, step, 0)

    def arrived(k, carry):
        ws_copy(k).wait_recv()
        wf_copy(k).wait_recv()
        return carry

    lax.fori_loop(0, chunks, arrived, 0)

    for t in range(tiles):
        key = pair_key[t]
        for u in range(units):
            at = jnp.where(key % units == u, key // units, MBLK)
            stacked[t, :, u * width:(u + 1) * width] = weighted[at]
    total = jnp.zeros((2 * block, units * width), jnp.float32)
    for t in range(tiles):
        total += jnp.dot(flipped[t], stacked[t], preferred_element_type=jnp.float32)

    power_sum = jnp.sum(info[:, rows_per:, :], axis=0)
    power_sum = jnp.sum(jnp.sum(power_sum, axis=1, keepdims=True), axis=0, keepdims=True)
    coefficient = reg_weight * power_sum / SPEAKERS
    for u in range(units):
        straight = total[:block, u * width:(u + 1) * width]
        crossed = pltpu.roll(total[block:, u * width:(u + 1) * width], half, 1)
        crossed = jnp.where(lane < half, crossed, -crossed)
        out[u] = straight + crossed + coefficient * direction[u]

    for j in range(1, group):
        info_copy(j).wait_send()

    def sent(k, carry):
        sib_copy(k).wait_send()
        y_copy(k).wait_send()
        ws_copy(k).wait_send()
        wy_copy(k).wait_send()
        wf_copy(k).wait_send()

        @pl.when(has_right)
        def _():
            right_copy(k).wait_send()

        @pl.when(has_left)
        def _():
            left_copy(k).wait_send()

        return carry

    lax.fori_loop(0, chunks, sent, 0)


def per_device(direction, plant, tile_pairs, mic_weight):
    device_id = lax.axis_index("spk")
    units, block, width = direction.shape
    tiles = plant.shape[0]
    bins = mic_weight.shape[0]
    group = SBLK // units
    quarter = MBLK // 4
    chunks = quarter // CHUNK
    rows_per = MBLK // group

    if bins == 1:
        weights = mic_weight.reshape(rows_per, block)
    else:
        whole = lax.all_gather(mic_weight, "spk", axis=1, tiled=True)
        weights = lax.dynamic_slice(
            whole, (device_id // group, (device_id % group) * rows_per, 0), (1, rows_per, block)
        )[0]

    unit = tile_pairs[:, 0] % units
    pair_key = tile_pairs[:, 1] * units + unit
    last = tiles * units
    slot = jnp.arange(tiles, dtype=jnp.int32) * units + unit
    hit = pair_key[:, None] == jnp.arange(MBLK * units, dtype=jnp.int32)[None, :]
    fwd_idx = last - jnp.sum(jnp.where(hit, (last - slot)[:, None], 0), axis=0)

    bf16, f32 = jnp.bfloat16, jnp.float32
    dma = pltpu.SemaphoreType.DMA
    vmem = pl.BlockSpec(memory_space=pltpu.VMEM)
    hbm = pl.BlockSpec(memory_space=pl.ANY)
    smem = pl.BlockSpec(memory_space=pltpu.SMEM)
    piece = (chunks, CHUNK, block, width)
    double = (chunks, 2 * CHUNK, block, width)
    return pl.pallas_call(
        functools.partial(kernel, group),
        out_shape=jax.ShapeDtypeStruct(direction.shape, f32),
        in_specs=[smem, smem, hbm, hbm, hbm],
        out_specs=vmem,
        scratch_shapes=[
            pltpu.VMEM(direction.shape, f32),
            pltpu.VMEM(plant.shape, bf16),
            pltpu.VMEM(weights.shape, f32),
            pltpu.VMEM((group, rows_per + 8, block), f32),
            pltpu.VMEM((tiles * units + 1, block, width), f32),
            pltpu.VMEM((tiles, 2 * block, block), bf16),
            pltpu.VMEM((2 * block, units * width), bf16),
            pltpu.VMEM(double, bf16),
            pltpu.VMEM(double, bf16),
            pltpu.VMEM(double, f32),
            pltpu.VMEM(piece, bf16),
            pltpu.VMEM(piece, bf16),
            pltpu.VMEM(piece, bf16),
            pltpu.VMEM(piece, bf16),
            pltpu.VMEM(piece, bf16),
            pltpu.VMEM(piece, bf16),
            pltpu.VMEM((MBLK + 1, block, width), bf16),
            pltpu.VMEM((tiles, block, units * width), bf16),
            dma((3,)), dma((group,)), dma((group,)),
        ] + [dma((chunks,)) for _ in range(14)],
        compiler_params=pltpu.CompilerParams(
            collective_id=0, has_side_effects=True, vmem_limit_bytes=60 * 1024 * 1024
        ),
        name="pressure_matching",
    )(fwd_idx, pair_key, direction, plant, weights)


def solution(mesh):
    placed = (
        P(("band", "spk"), None, None),
        P(("band", "spk"), None, None, None),
        P(("band", "spk"), None),
        P("band", "spk", None),
    )
    return jax.shard_map(
        per_device,
        mesh=mesh,
        in_specs=placed,
        out_specs=P(("band", "spk"), None, None),
        check_vma=False,
    )
```

```python
import functools

import jax
import jax.numpy as jnp
from jax import lax
from jax.experimental import pallas as pl
from jax.experimental.pallas import tpu as pltpu
from jax.sharding import PartitionSpec as P

SBLK = 32
MBLK = 128
SPEAKERS = 4096
CHUNKS = 16
LAG = 2

reg_weight = 0.25

MESH = pl.DeviceIdType.MESH


def kernel(
    group, fwd_idx, pair_key, direction_in, plant_in, weights_in, out,
    direction, plant, weights, info, products, flipped, fields, sib_out, sib_in, own,
    y_out, y_in, right_out, left_out, from_left, from_right,
    root_out, root_left, root_right, swap_out, swap_in, weighted, stacked,
    load_s, info_s, info_r, sends,
    sib_r, y_r, right_r, left_r, wy_r, toward_right_r, toward_left_r, swap_r, spread_r, ends_r,
):
    units, block, width = direction.shape
    tiles = plant.shape[0]
    column = MBLK // 8
    square = MBLK // 4
    per_a = column // CHUNKS
    per_b = square // CHUNKS
    rows_per = MBLK // group
    depth = group // 4
    reach = depth // 2
    half = width // 2

    me = lax.axis_index("spk")
    base = (me // group) * group
    rank = me - base
    z = rank // 4
    y = (rank // 2) % 2
    c = rank % 2
    sib = me + 1 - 2 * c
    other_y = me + 2 - 4 * y
    q_mine = y * 2 + c
    q_sib = y * 2 + 1 - c
    q_y = (1 - y) * 2 + c
    q_diag = (1 - y) * 2 + 1 - c
    wide_mine = MBLK // 2 + c * square
    wide_sib = MBLK // 2 + (1 - c) * square
    has_left = z > 0
    has_right = z < depth - 1

    def peer(j):
        return base + (rank + j) % group

    def copy(src, dst, send, recv, device):
        return pltpu.make_async_remote_copy(
            src_ref=src, dst_ref=dst, send_sem=send, recv_sem=recv,
            device_id={"spk": device}, device_id_type=MESH,
        )

    loads = [
        pltpu.make_async_copy(src, dst, load_s.at[n])
        for n, (src, dst) in enumerate(
            [(direction_in, direction), (plant_in, plant), (weights_in, weights)]
        )
    ]
    for load in loads:
        load.start()
    barrier = pltpu.get_barrier_semaphore()
    for j in range(1, group):
        pl.semaphore_signal(barrier, inc=1, device_id={"spk": peer(j)}, device_id_type=MESH)

    loads[0].wait()
    lane = lax.broadcasted_iota(jnp.int32, (block, width), 1)
    for u in range(units):
        x = direction[u]
        turned = pltpu.roll(x, half, 1)
        turned = jnp.where(lane < half, -turned, turned)
        fields[:block, u * width:(u + 1) * width] = x.astype(jnp.bfloat16)
        fields[block:, u * width:(u + 1) * width] = turned.astype(jnp.bfloat16)
    loads[1].wait()

    def pack(t, power):
        p0 = plant[t, 0]
        p1 = plant[t, 1]
        both = jnp.dot(
            jnp.concatenate([p0, p1], axis=1), fields[...], preferred_element_type=jnp.float32
        )
        for u in range(units):
            products[t * units + u] = both[:, u * width:(u + 1) * width]
        f0 = p0.astype(jnp.float32)
        f1 = p1.astype(jnp.float32)
        squares = f0 * f0 + f1 * f1
        return power + jnp.sum(squares.reshape(block // 8, 8, block), axis=0)

    power = lax.fori_loop(0, tiles, pack, jnp.zeros((8, block), jnp.float32))
    products[tiles * units] = jnp.zeros((block, width), jnp.float32)
    weighted[MBLK] = jnp.zeros((block, width), jnp.bfloat16)
    loads[2].wait()
    info[rank, :rows_per, :] = weights[...]
    info[rank, rows_per:, :] = power

    pl.semaphore_wait(barrier, group - 1)

    def info_copy(j):
        return copy(info.at[rank], info.at[rank], info_s.at[j], info_r.at[j], peer(j))

    def part(q, k):
        return weighted.at[pl.ds(q * column + k * per_a, per_a)]

    def wide(first, k):
        return weighted.at[pl.ds(first + k * per_b, per_b)]

    def sib_copy(k):
        return copy(sib_out.at[k], sib_in.at[k], sends.at[0], sib_r.at[k], sib)

    def y_copy(k):
        return copy(y_out.at[k], y_in.at[k], sends.at[1], y_r.at[k], other_y)

    def right_copy(k):
        return copy(right_out.at[k], from_left.at[k], sends.at[2], right_r.at[k], me + 4)

    def left_copy(k):
        return copy(left_out.at[k], from_right.at[k], sends.at[3], left_r.at[k], me - 4)

    def wy_copy(k):
        return copy(part(q_mine, k), part(q_mine, k), sends.at[4], wy_r.at[k], other_y)

    def ws_copy(k):
        return copy(part(q_mine, k), part(q_mine, k), sends.at[5], ends_r.at[0], sib)

    def wf_copy(k):
        return copy(part(q_y, k), part(q_y, k), sends.at[6], ends_r.at[1], sib)

    def wide_copy(k):
        return copy(wide(wide_mine, k), wide(wide_mine, k), sends.at[7], ends_r.at[2], sib)

    def toward_right(k):
        return copy(root_out.at[k], root_left.at[k], sends.at[8], toward_right_r.at[k], me + 4)

    def toward_left(k):
        return copy(root_out.at[k], root_right.at[k], sends.at[9], toward_left_r.at[k], me - 4)

    def swap_copy(k):
        return copy(swap_out.at[k], swap_in.at[k], sends.at[10], swap_r.at[k], other_y)

    def spread_right(k):
        return copy(wide(wide_mine, k), wide(wide_mine, k), sends.at[11], spread_r.at[k], me + 4)

    def spread_left(k):
        return copy(wide(wide_mine, k), wide(wide_mine, k), sends.at[12], spread_r.at[k], me - 4)

    for j in range(1, group):
        info_copy(j).start()

    def product(v):
        total = products[fwd_idx[v * units]]
        for u in range(1, units):
            total += products[fwd_idx[v * units + u]]
        return total

    def inside(k):
        return jnp.logical_and(k >= 0, k < CHUNKS)

    def scaled(v, pressure):
        row = info[v // rows_per, pl.ds(v % rows_per, 1), :]
        scale = jnp.broadcast_to(row, (block, block)).T
        weighted[v] = (scale * pressure).astype(jnp.bfloat16)

    def root_of(k):
        return reach - 1 + k % 2

    def step(s, carry):
        @pl.when(inside(s))
        def _():
            k = s
            for i in range(per_a):
                at = k * per_a + i
                sib_out[k, i] = product(q_sib * column + at).astype(jnp.bfloat16)
                sib_out[k, per_a + i] = product(q_diag * column + at).astype(jnp.bfloat16)
            for i in range(per_b):
                at = k * per_b + i
                sib_out[k, 2 * per_a + i] = product(wide_sib + at).astype(jnp.bfloat16)
            sib_copy(k).start()
            for i in range(per_a):
                at = k * per_a + i
                own[k, i] = product(q_mine * column + at)
                own[k, per_a + i] = product(q_y * column + at)
            for i in range(per_b):
                own[k, 2 * per_a + i] = product(wide_mine + k * per_b + i)

        k1 = s - LAG

        @pl.when(inside(k1))
        def _():
            sib_copy(k1).wait_recv()
            for i in range(per_a):
                total = own[k1, per_a + i] + sib_in[k1, per_a + i].astype(jnp.float32)
                y_out[k1, i] = total.astype(jnp.bfloat16)
            y_copy(k1).start()
            for i in range(per_a):
                own[k1, i] = own[k1, i] + sib_in[k1, i].astype(jnp.float32)
            for i in range(2 * per_a, 2 * per_a + per_b):
                own[k1, i] = own[k1, i] + sib_in[k1, i].astype(jnp.float32)

        for d in range(reach, 0, -1):
            kb = s - LAG * (1 + reach - d)
            gap = z - root_of(kb)

            @pl.when(jnp.logical_and(inside(kb), gap == -d))
            def _():
                @pl.when(has_left)
                def _():
                    toward_right(kb).wait_recv()
                    for i in range(per_b):
                        total = own[kb, 2 * per_a + i] + root_left[kb, i].astype(jnp.float32)
                        root_out[kb, i] = total.astype(jnp.bfloat16)

                @pl.when(jnp.logical_not(has_left))
                def _():
                    for i in range(per_b):
                        root_out[kb, i] = own[kb, 2 * per_a + i].astype(jnp.bfloat16)

                toward_right(kb).start()

            @pl.when(jnp.logical_and(inside(kb), gap == d))
            def _():
                @pl.when(has_right)
                def _():
                    toward_left(kb).wait_recv()
                    for i in range(per_b):
                        total = own[kb, 2 * per_a + i] + root_right[kb, i].astype(jnp.float32)
                        root_out[kb, i] = total.astype(jnp.bfloat16)

                @pl.when(jnp.logical_not(has_right))
                def _():
                    for i in range(per_b):
                        root_out[kb, i] = own[kb, 2 * per_a + i].astype(jnp.bfloat16)

                toward_left(kb).start()

        k2 = s - 2 * LAG

        @pl.when(inside(k2))
        def _():
            y_copy(k2).wait_recv()
            for i in range(per_a):
                own[k2, i] = own[k2, i] + y_in[k2, i].astype(jnp.float32)

        kr = s - LAG * (2 + z)

        @pl.when(inside(kr))
        def _():
            @pl.when(has_left)
            def _():
                right_copy(kr).wait_recv()

            @pl.when(jnp.logical_and(has_left, has_right))
            def _():
                for i in range(per_a):
                    total = own[kr, i] + from_left[kr, i].astype(jnp.float32)
                    right_out[kr, i] = total.astype(jnp.bfloat16)

            @pl.when(jnp.logical_not(has_left))
            def _():
                for i in range(per_a):
                    right_out[kr, i] = own[kr, i].astype(jnp.bfloat16)

            @pl.when(has_right)
            def _():
                right_copy(kr).start()

        kl = s - LAG * (2 + depth - 1 - z)

        @pl.when(inside(kl))
        def _():
            @pl.when(has_right)
            def _():
                left_copy(kl).wait_recv()

            @pl.when(jnp.logical_and(has_left, has_right))
            def _():
                for i in range(per_a):
                    total = own[kl, i] + from_right[kl, i].astype(jnp.float32)
                    left_out[kl, i] = total.astype(jnp.bfloat16)

            @pl.when(jnp.logical_not(has_right))
            def _():
                for i in range(per_a):
                    left_out[kl, i] = own[kl, i].astype(jnp.bfloat16)

            @pl.when(has_left)
            def _():
                left_copy(kl).start()

        kc = s - LAG * (1 + reach)

        @pl.when(jnp.logical_and(inside(kc), z == root_of(kc)))
        def _():
            @pl.when(has_left)
            def _():
                toward_right(kc).wait_recv()
                for i in range(per_b):
                    at = 2 * per_a + i
                    own[kc, at] = own[kc, at] + root_left[kc, i].astype(jnp.float32)

            @pl.when(has_right)
            def _():
                toward_left(kc).wait_recv()
                for i in range(per_b):
                    at = 2 * per_a + i
                    own[kc, at] = own[kc, at] + root_right[kc, i].astype(jnp.float32)

            for i in range(per_b):
                swap_out[kc, i] = own[kc, 2 * per_a + i].astype(jnp.bfloat16)
            swap_copy(kc).start()

        @pl.when(s == LAG * (2 + reach))
        def _():
            for j in range(1, group):
                info_copy(j).wait_recv()

        kw = s - LAG * (2 + reach)

        @pl.when(jnp.logical_and(inside(kw), z == root_of(kw)))
        def _():
            swap_copy(kw).wait_recv()
            for i in range(per_b):
                total = own[kw, 2 * per_a + i] + swap_in[kw, i].astype(jnp.float32)
                scaled(wide_mine + kw * per_b + i, total)

            @pl.when(has_left)
            def _():
                spread_left(kw).start()

            @pl.when(has_right)
            def _():
                spread_right(kw).start()

            wide_copy(kw).start()

        for d in range(1, reach + 1):
            ko = s - LAG * (2 + reach + d)
            gap = z - root_of(ko)

            @pl.when(jnp.logical_and(inside(ko), gap == -d))
            def _():
                spread_left(ko).wait_recv()

                @pl.when(has_left)
                def _():
                    spread_left(ko).start()

                wide_copy(ko).start()

            @pl.when(jnp.logical_and(inside(ko), gap == d))
            def _():
                spread_right(ko).wait_recv()

                @pl.when(has_right)
                def _():
                    spread_right(ko).start()

                wide_copy(ko).start()

        kt = s - LAG * (2 + jnp.maximum(z, depth - 1 - z))

        @pl.when(inside(kt))
        def _():
            @pl.when(has_left)
            def _():
                for i in range(per_a):
                    own[kt, i] = own[kt, i] + from_left[kt, i].astype(jnp.float32)

            @pl.when(has_right)
            def _():
                for i in range(per_a):
                    own[kt, i] = own[kt, i] + from_right[kt, i].astype(jnp.float32)

            for i in range(per_a):
                scaled(q_mine * column + kt * per_a + i, own[kt, i])
            wy_copy(kt).start()
            ws_copy(kt).start()

        kd = kt - LAG

        @pl.when(inside(kd))
        def _():
            wy_copy(kd).wait_recv()
            wf_copy(kd).start()

        @pl.when(s < tiles)
        def _():
            flipped[s, :block, :] = plant[s, 0].T
            flipped[s, block:, :] = plant[s, 1].T

        return carry

    steps = max(CHUNKS + LAG * max(depth + 2, 2 + 2 * reach), tiles)
    lax.fori_loop(0, steps, step, 0)

    def whole_part(q):
        return weighted.at[pl.ds(q * column, column)]

    def whole_wide(first, amount):
        return weighted.at[pl.ds(first, amount)]

    def all_of(src, send, recv):
        return copy(src, src, sends.at[send], ends_r.at[recv], sib)

    all_of(whole_part(q_sib), 5, 0).wait_recv()
    all_of(whole_part(q_diag), 6, 1).wait_recv()
    all_of(whole_wide(wide_sib, square), 7, 2).wait_recv()

    for t in range(tiles):
        key = pair_key[t]
        for u in range(units):
            at = jnp.where(key % units == u, key // units, MBLK)
            stacked[t, :, u * width:(u + 1) * width] = weighted[at]
    total = jnp.zeros((2 * block, units * width), jnp.float32)
    for t in range(tiles):
        total += jnp.dot(flipped[t], stacked[t], preferred_element_type=jnp.float32)

    power_sum = jnp.sum(info[:, rows_per:, :], axis=0)
    power_sum = jnp.sum(jnp.sum(power_sum, axis=1, keepdims=True), axis=0, keepdims=True)
    coefficient = reg_weight * power_sum / SPEAKERS
    for u in range(units):
        straight = total[:block, u * width:(u + 1) * width]
        crossed = pltpu.roll(total[block:, u * width:(u + 1) * width], half, 1)
        crossed = jnp.where(lane < half, crossed, -crossed)
        out[u] = straight + crossed + coefficient * direction[u]

    for j in range(1, group):
        info_copy(j).wait_send()

    all_of(sib_out, 0, 0).wait_send()
    all_of(y_out, 1, 0).wait_send()
    all_of(whole_part(q_mine), 4, 0).wait_send()
    all_of(whole_part(q_mine), 5, 0).wait_send()
    all_of(whole_part(q_y), 6, 0).wait_send()
    all_of(whole_wide(wide_mine, square), 7, 0).wait_send()

    @pl.when(has_right)
    def _():
        all_of(right_out, 2, 0).wait_send()

    @pl.when(has_left)
    def _():
        all_of(left_out, 3, 0).wait_send()

    some = square // 2

    @pl.when(z < reach - 1)
    def _():
        all_of(whole_wide(wide_mine, square), 8, 0).wait_send()

    @pl.when(z == reach - 1)
    def _():
        all_of(whole_wide(wide_mine, some), 8, 0).wait_send()
        all_of(whole_wide(wide_mine, some), 10, 0).wait_send()
        all_of(whole_wide(wide_mine, some), 11, 0).wait_send()

    @pl.when(z > reach)
    def _():
        all_of(whole_wide(wide_mine, square), 9, 0).wait_send()

    @pl.when(z == reach)
    def _():
        all_of(whole_wide(wide_mine, some), 9, 0).wait_send()
        all_of(whole_wide(wide_mine, some), 10, 0).wait_send()
        all_of(whole_wide(wide_mine, some), 12, 0).wait_send()

    @pl.when(jnp.logical_and(z >= reach, has_right))
    def _():
        all_of(whole_wide(wide_mine, square), 11, 0).wait_send()

    @pl.when(jnp.logical_and(z < reach, has_left))
    def _():
        all_of(whole_wide(wide_mine, square), 12, 0).wait_send()


def per_device(direction, plant, tile_pairs, mic_weight):
    device_id = lax.axis_index("spk")
    units, block, width = direction.shape
    tiles = plant.shape[0]
    bins = mic_weight.shape[0]
    group = SBLK // units
    per_a = MBLK // 8 // CHUNKS
    per_b = MBLK // 4 // CHUNKS
    rows_per = MBLK // group

    if bins == 1:
        weights = mic_weight.reshape(rows_per, block)
    else:
        whole = lax.all_gather(mic_weight, "spk", axis=1, tiled=True)
        weights = lax.dynamic_slice(
            whole, (device_id // group, (device_id % group) * rows_per, 0), (1, rows_per, block)
        )[0]

    unit = tile_pairs[:, 0] % units
    pair_key = tile_pairs[:, 1] * units + unit
    last = tiles * units
    slot = jnp.arange(tiles, dtype=jnp.int32) * units + unit
    hit = pair_key[:, None] == jnp.arange(MBLK * units, dtype=jnp.int32)[None, :]
    fwd_idx = last - jnp.sum(jnp.where(hit, (last - slot)[:, None], 0), axis=0)

    bf16, f32 = jnp.bfloat16, jnp.float32
    dma = pltpu.SemaphoreType.DMA
    vmem = pl.BlockSpec(memory_space=pltpu.VMEM)
    hbm = pl.BlockSpec(memory_space=pl.ANY)
    smem = pl.BlockSpec(memory_space=pltpu.SMEM)
    piece = (CHUNKS, per_a, block, width)
    large = (CHUNKS, per_b, block, width)
    mixed = (CHUNKS, 2 * per_a + per_b, block, width)
    return pl.pallas_call(
        functools.partial(kernel, group),
        out_shape=jax.ShapeDtypeStruct(direction.shape, f32),
        in_specs=[smem, smem, hbm, hbm, hbm],
        out_specs=vmem,
        scratch_shapes=[
            pltpu.VMEM(direction.shape, f32),
            pltpu.VMEM(plant.shape, bf16),
            pltpu.VMEM(weights.shape, f32),
            pltpu.VMEM((group, rows_per + 8, block), f32),
            pltpu.VMEM((tiles * units + 1, block, width), f32),
            pltpu.VMEM((tiles, 2 * block, block), bf16),
            pltpu.VMEM((2 * block, units * width), bf16),
            pltpu.VMEM(mixed, bf16),
            pltpu.VMEM(mixed, bf16),
            pltpu.VMEM(mixed, f32),
        ] + [pltpu.VMEM(piece, bf16)] * 6 + [pltpu.VMEM(large, bf16)] * 5 + [
            pltpu.VMEM((MBLK + 1, block, width), bf16),
            pltpu.VMEM((tiles, block, units * width), bf16),
            dma((3,)), dma((group,)), dma((group,)), dma((13,)),
        ] + [dma((CHUNKS,))] * 9 + [dma((3,))],
        compiler_params=pltpu.CompilerParams(
            collective_id=0, has_side_effects=True, vmem_limit_bytes=60 * 1024 * 1024
        ),
        name="pressure_matching",
    )(fwd_idx, pair_key, direction, plant, weights)


def solution(mesh):
    placed = (
        P(("band", "spk"), None, None),
        P(("band", "spk"), None, None, None),
        P(("band", "spk"), None),
        P("band", "spk", None),
    )
    return jax.shard_map(
        per_device,
        mesh=mesh,
        in_specs=placed,
        out_specs=P(("band", "spk"), None, None),
        check_vma=False,
    )
```

```python
import functools

import jax
import jax.numpy as jnp
from jax import lax
from jax.experimental import pallas as pl
from jax.experimental.pallas import tpu as pltpu
from jax.sharding import PartitionSpec as P

SBLK = 32
MBLK = 128
SPEAKERS = 4096
CHUNKS = 16
LAG = 2

reg_weight = 0.25

MESH = pl.DeviceIdType.MESH


def kernel(
    group, pairs, direction_in, plant_in, weights_in, out,
    direction, plant, weights, info, power, table, slots, products, flipped, fields, sib_out, sib_in, own,
    y_out, y_in, right_out, left_out, from_left, from_right,
    root_out, root_left, root_right, swap_out, swap_in, weighted, stacked,
    load_s, info_s, info_r, power_s, power_r, sends,
    sib_r, y_r, right_r, left_r, wy_r, toward_right_r, toward_left_r, swap_r, spread_r, ends_r,
):
    units, block, width = direction.shape
    tiles = plant.shape[0]
    column = MBLK // 8
    square = MBLK // 4
    per_a = column // CHUNKS
    per_b = square // CHUNKS
    rows_per = MBLK // group
    depth = group // 4
    reach = depth // 2
    half = width // 2

    me = lax.axis_index("spk")
    base = (me // group) * group
    rank = me - base
    z = rank // 4
    y = (rank // 2) % 2
    c = rank % 2
    sib = me + 1 - 2 * c
    other_y = me + 2 - 4 * y
    q_mine = y * 2 + c
    q_sib = y * 2 + 1 - c
    q_y = (1 - y) * 2 + c
    q_diag = (1 - y) * 2 + 1 - c
    wide_mine = MBLK // 2 + c * square
    wide_sib = MBLK // 2 + (1 - c) * square
    has_left = z > 0
    has_right = z < depth - 1

    def peer(j):
        return base + (rank + j) % group

    def copy(src, dst, send, recv, device):
        return pltpu.make_async_remote_copy(
            src_ref=src, dst_ref=dst, send_sem=send, recv_sem=recv,
            device_id={"spk": device}, device_id_type=MESH,
        )

    loads = [
        pltpu.make_async_copy(src, dst, load_s.at[n])
        for n, (src, dst) in enumerate(
            [(direction_in, direction), (plant_in, plant), (weights_in, weights)]
        )
    ]
    for load in loads:
        load.start()
    barrier = pltpu.get_barrier_semaphore()
    for j in range(1, group):
        pl.semaphore_signal(barrier, inc=1, device_id={"spk": peer(j)}, device_id_type=MESH)

    row_id = lax.broadcasted_iota(jnp.int32, (8, MBLK), 0)
    lane_id = lax.broadcasted_iota(jnp.int32, (8, MBLK), 1)
    found = jnp.full((8, MBLK), tiles * units, jnp.int32)
    for t in range(tiles):
        u = pairs[0, t] % units
        hit = jnp.logical_and(row_id == u, lane_id == pairs[1, t])
        found = jnp.where(hit, t * units + u, found)
    table[...] = found
    to_slots = pltpu.make_async_copy(table, slots, load_s.at[3])
    to_slots.start()

    loads[0].wait()
    lane = lax.broadcasted_iota(jnp.int32, (block, width), 1)
    for u in range(units):
        x = direction[u]
        turned = pltpu.roll(x, half, 1)
        turned = jnp.where(lane < half, -turned, turned)
        fields[:block, u * width:(u + 1) * width] = x.astype(jnp.bfloat16)
        fields[block:, u * width:(u + 1) * width] = turned.astype(jnp.bfloat16)
    loads[1].wait()

    def multiply(t, carry):
        both = jnp.dot(
            jnp.concatenate([plant[t, 0], plant[t, 1]], axis=1),
            fields[...],
            preferred_element_type=jnp.float32,
        )
        for u in range(units):
            products[t * units + u] = both[:, u * width:(u + 1) * width]
        return carry

    lax.fori_loop(0, tiles, multiply, 0, unroll=2)
    products[tiles * units] = jnp.zeros((block, width), jnp.float32)
    weighted[MBLK] = jnp.zeros((block, width), jnp.bfloat16)
    loads[2].wait()
    info[rank] = weights[...]
    power[rank] = jnp.zeros((8, block), jnp.float32)
    to_slots.wait()

    pl.semaphore_wait(barrier, group - 1)

    def info_copy(j):
        return copy(info.at[rank], info.at[rank], info_s.at[j], info_r.at[j], peer(j))

    def part(q, k):
        return weighted.at[pl.ds(q * column + k * per_a, per_a)]

    def wide(first, k):
        return weighted.at[pl.ds(first + k * per_b, per_b)]

    def power_copy(j):
        return copy(power.at[rank], power.at[rank], power_s.at[j], power_r.at[j], peer(j))

    def sib_copy(k):
        return copy(sib_out.at[k], sib_in.at[k], sends.at[0], sib_r.at[k], sib)

    def y_copy(k):
        return copy(y_out.at[k], y_in.at[k], sends.at[1], y_r.at[k], other_y)

    def right_copy(k):
        return copy(right_out.at[k], from_left.at[k], sends.at[2], right_r.at[k], me + 4)

    def left_copy(k):
        return copy(left_out.at[k], from_right.at[k], sends.at[3], left_r.at[k], me - 4)

    def wy_copy(k):
        return copy(part(q_mine, k), part(q_mine, k), sends.at[4], wy_r.at[k], other_y)

    def ws_copy(k):
        return copy(part(q_mine, k), part(q_mine, k), sends.at[5], ends_r.at[0], sib)

    def wf_copy(k):
        return copy(part(q_y, k), part(q_y, k), sends.at[6], ends_r.at[1], sib)

    def wide_copy(k):
        return copy(wide(wide_mine, k), wide(wide_mine, k), sends.at[7], ends_r.at[2], sib)

    def toward_right(k):
        return copy(root_out.at[k], root_left.at[k], sends.at[8], toward_right_r.at[k], me + 4)

    def toward_left(k):
        return copy(root_out.at[k], root_right.at[k], sends.at[9], toward_left_r.at[k], me - 4)

    def swap_copy(k):
        return copy(swap_out.at[k], swap_in.at[k], sends.at[10], swap_r.at[k], other_y)

    def spread_right(k):
        return copy(wide(wide_mine, k), wide(wide_mine, k), sends.at[11], spread_r.at[k], me + 4)

    def spread_left(k):
        return copy(wide(wide_mine, k), wide(wide_mine, k), sends.at[12], spread_r.at[k], me - 4)

    for j in range(1, group):
        info_copy(j).start()

    def product(v):
        total = products[slots[0, v]]
        for u in range(1, units):
            total += products[slots[u, v]]
        return total

    def inside(k):
        return jnp.logical_and(k >= 0, k < CHUNKS)

    def scaled(v, pressure):
        row = info[v // rows_per, pl.ds(v % rows_per, 1), :]
        scale = jnp.broadcast_to(row, (block, block)).T
        weighted[v] = (scale * pressure).astype(jnp.bfloat16)

    def root_of(k):
        return reach - 1 + k % 2

    first = 6

    def step(s, carry):
        @pl.when(inside(s))
        def _():
            k = s
            for i in range(per_a):
                at = k * per_a + i
                sib_out[k, i] = product(q_sib * column + at).astype(jnp.bfloat16)
                sib_out[k, per_a + i] = product(q_diag * column + at).astype(jnp.bfloat16)
            for i in range(per_b):
                at = k * per_b + i
                sib_out[k, 2 * per_a + i] = product(wide_sib + at).astype(jnp.bfloat16)
            sib_copy(k).start()

        k1 = s - LAG

        @pl.when(inside(k1))
        def _():
            sib_copy(k1).wait_recv()
            for i in range(per_a):
                total = product(q_y * column + k1 * per_a + i)
                total += sib_in[k1, per_a + i].astype(jnp.float32)
                y_out[k1, i] = total.astype(jnp.bfloat16)
            y_copy(k1).start()
            for i in range(per_b):
                at = per_a + i
                total = product(wide_mine + k1 * per_b + i)
                own[k1, at] = total + sib_in[k1, per_a + at].astype(jnp.float32)
            for i in range(per_a):
                total = product(q_mine * column + k1 * per_a + i)
                own[k1, i] = total + sib_in[k1, i].astype(jnp.float32)

        for d in range(reach, 0, -1):
            kb = s - LAG * (1 + reach - d)
            gap = z - root_of(kb)

            @pl.when(jnp.logical_and(inside(kb), gap == -d))
            def _():
                @pl.when(has_left)
                def _():
                    toward_right(kb).wait_recv()
                    for i in range(per_b):
                        total = own[kb, per_a + i] + root_left[kb, i].astype(jnp.float32)
                        root_out[kb, i] = total.astype(jnp.bfloat16)

                @pl.when(jnp.logical_not(has_left))
                def _():
                    for i in range(per_b):
                        root_out[kb, i] = own[kb, per_a + i].astype(jnp.bfloat16)

                toward_right(kb).start()

            @pl.when(jnp.logical_and(inside(kb), gap == d))
            def _():
                @pl.when(has_right)
                def _():
                    toward_left(kb).wait_recv()
                    for i in range(per_b):
                        total = own[kb, per_a + i] + root_right[kb, i].astype(jnp.float32)
                        root_out[kb, i] = total.astype(jnp.bfloat16)

                @pl.when(jnp.logical_not(has_right))
                def _():
                    for i in range(per_b):
                        root_out[kb, i] = own[kb, per_a + i].astype(jnp.bfloat16)

                toward_left(kb).start()

        k2 = s - 2 * LAG

        @pl.when(inside(k2))
        def _():
            y_copy(k2).wait_recv()
            for i in range(per_a):
                own[k2, i] = own[k2, i] + y_in[k2, i].astype(jnp.float32)

        kr = s - LAG * (2 + z)

        @pl.when(inside(kr))
        def _():
            @pl.when(has_left)
            def _():
                right_copy(kr).wait_recv()

            @pl.when(jnp.logical_and(has_left, has_right))
            def _():
                for i in range(per_a):
                    total = own[kr, i] + from_left[kr, i].astype(jnp.float32)
                    right_out[kr, i] = total.astype(jnp.bfloat16)

            @pl.when(jnp.logical_not(has_left))
            def _():
                for i in range(per_a):
                    right_out[kr, i] = own[kr, i].astype(jnp.bfloat16)

            @pl.when(has_right)
            def _():
                right_copy(kr).start()

        kl = s - LAG * (2 + depth - 1 - z)

        @pl.when(inside(kl))
        def _():
            @pl.when(has_right)
            def _():
                left_copy(kl).wait_recv()

            @pl.when(jnp.logical_and(has_left, has_right))
            def _():
                for i in range(per_a):
                    total = own[kl, i] + from_right[kl, i].astype(jnp.float32)
                    left_out[kl, i] = total.astype(jnp.bfloat16)

            @pl.when(jnp.logical_not(has_right))
            def _():
                for i in range(per_a):
                    left_out[kl, i] = own[kl, i].astype(jnp.bfloat16)

            @pl.when(has_left)
            def _():
                left_copy(kl).start()

        kc = s - LAG * (1 + reach)

        @pl.when(jnp.logical_and(inside(kc), z == root_of(kc)))
        def _():
            @pl.when(has_left)
            def _():
                toward_right(kc).wait_recv()
                for i in range(per_b):
                    at = per_a + i
                    own[kc, at] = own[kc, at] + root_left[kc, i].astype(jnp.float32)

            @pl.when(has_right)
            def _():
                toward_left(kc).wait_recv()
                for i in range(per_b):
                    at = per_a + i
                    own[kc, at] = own[kc, at] + root_right[kc, i].astype(jnp.float32)

            for i in range(per_b):
                swap_out[kc, i] = own[kc, per_a + i].astype(jnp.bfloat16)
            swap_copy(kc).start()

        @pl.when(s == LAG * (2 + reach))
        def _():
            for j in range(1, group):
                info_copy(j).wait_recv()

        kw = s - LAG * (2 + reach)

        @pl.when(jnp.logical_and(inside(kw), z == root_of(kw)))
        def _():
            swap_copy(kw).wait_recv()
            for i in range(per_b):
                total = own[kw, per_a + i] + swap_in[kw, i].astype(jnp.float32)
                scaled(wide_mine + kw * per_b + i, total)

            @pl.when(has_left)
            def _():
                spread_left(kw).start()

            @pl.when(has_right)
            def _():
                spread_right(kw).start()

            wide_copy(kw).start()

        for d in range(1, reach + 1):
            ko = s - LAG * (2 + reach + d)
            gap = z - root_of(ko)

            @pl.when(jnp.logical_and(inside(ko), gap == -d))
            def _():
                spread_left(ko).wait_recv()

                @pl.when(has_left)
                def _():
                    spread_left(ko).start()

                wide_copy(ko).start()

            @pl.when(jnp.logical_and(inside(ko), gap == d))
            def _():
                spread_right(ko).wait_recv()

                @pl.when(has_right)
                def _():
                    spread_right(ko).start()

                wide_copy(ko).start()

        kt = s - LAG * (2 + jnp.maximum(z, depth - 1 - z))

        @pl.when(inside(kt))
        def _():
            @pl.when(has_left)
            def _():
                for i in range(per_a):
                    own[kt, i] = own[kt, i] + from_left[kt, i].astype(jnp.float32)

            @pl.when(has_right)
            def _():
                for i in range(per_a):
                    own[kt, i] = own[kt, i] + from_right[kt, i].astype(jnp.float32)

            for i in range(per_a):
                scaled(q_mine * column + kt * per_a + i, own[kt, i])
            wy_copy(kt).start()
            ws_copy(kt).start()

        kd = kt - LAG

        @pl.when(inside(kd))
        def _():
            wy_copy(kd).wait_recv()
            wf_copy(kd).start()

        n = s - first

        @pl.when(jnp.logical_and(n >= 0, n < tiles // 2))
        def _():
            squares = power[rank]
            for m in range(2):
                p0 = plant[2 * n + m, 0]
                p1 = plant[2 * n + m, 1]
                flipped[n, :block, m * block:(m + 1) * block] = p0.T
                flipped[n, block:, m * block:(m + 1) * block] = p1.T
                f0 = p0.astype(jnp.float32)
                f1 = p1.astype(jnp.float32)
                both = f0 * f0 + f1 * f1
                squares += jnp.sum(both.reshape(block // 8, 8, block), axis=0)
            power[rank] = squares

        @pl.when(n == tiles // 2)
        def _():
            for j in range(1, group):
                power_copy(j).start()

        return carry

    steps = max(CHUNKS + LAG * max(depth + 2, 2 + 2 * reach), first + tiles // 2 + 1)
    lax.fori_loop(0, steps, step, 0)

    def whole_part(q):
        return weighted.at[pl.ds(q * column, column)]

    def whole_wide(first, amount):
        return weighted.at[pl.ds(first, amount)]

    def all_of(src, send, recv):
        return copy(src, src, sends.at[send], ends_r.at[recv], sib)

    all_of(whole_part(q_sib), 5, 0).wait_recv()
    all_of(whole_part(q_diag), 6, 1).wait_recv()
    all_of(whole_wide(wide_sib, square), 7, 2).wait_recv()

    for t in range(tiles):
        unit = pairs[0, t] % units
        rows = slice((t % 2) * block, (t % 2 + 1) * block)
        for u in range(units):
            at = jnp.where(unit == u, pairs[1, t], MBLK)
            stacked[t // 2, rows, u * width:(u + 1) * width] = weighted[at]
    total = jnp.zeros((2 * block, units * width), jnp.float32)
    for n in range(tiles // 2):
        total += jnp.dot(flipped[n], stacked[n], preferred_element_type=jnp.float32)

    for j in range(1, group):
        power_copy(j).wait_recv()
    power_sum = jnp.sum(power[...], axis=0)
    power_sum = jnp.sum(jnp.sum(power_sum, axis=1, keepdims=True), axis=0, keepdims=True)
    coefficient = reg_weight * power_sum / SPEAKERS
    for u in range(units):
        straight = total[:block, u * width:(u + 1) * width]
        crossed = pltpu.roll(total[block:, u * width:(u + 1) * width], half, 1)
        crossed = jnp.where(lane < half, crossed, -crossed)
        out[u] = straight + crossed + coefficient * direction[u]

    for j in range(1, group):
        info_copy(j).wait_send()
        power_copy(j).wait_send()

    all_of(sib_out, 0, 0).wait_send()
    all_of(y_out, 1, 0).wait_send()
    all_of(whole_part(q_mine), 4, 0).wait_send()
    all_of(whole_part(q_mine), 5, 0).wait_send()
    all_of(whole_part(q_y), 6, 0).wait_send()
    all_of(whole_wide(wide_mine, square), 7, 0).wait_send()

    @pl.when(has_right)
    def _():
        all_of(right_out, 2, 0).wait_send()

    @pl.when(has_left)
    def _():
        all_of(left_out, 3, 0).wait_send()

    some = square // 2

    @pl.when(z < reach - 1)
    def _():
        all_of(whole_wide(wide_mine, square), 8, 0).wait_send()

    @pl.when(z == reach - 1)
    def _():
        all_of(whole_wide(wide_mine, some), 8, 0).wait_send()
        all_of(whole_wide(wide_mine, some), 10, 0).wait_send()
        all_of(whole_wide(wide_mine, some), 11, 0).wait_send()

    @pl.when(z > reach)
    def _():
        all_of(whole_wide(wide_mine, square), 9, 0).wait_send()

    @pl.when(z == reach)
    def _():
        all_of(whole_wide(wide_mine, some), 9, 0).wait_send()
        all_of(whole_wide(wide_mine, some), 10, 0).wait_send()
        all_of(whole_wide(wide_mine, some), 12, 0).wait_send()

    @pl.when(jnp.logical_and(z >= reach, has_right))
    def _():
        all_of(whole_wide(wide_mine, square), 11, 0).wait_send()

    @pl.when(jnp.logical_and(z < reach, has_left))
    def _():
        all_of(whole_wide(wide_mine, square), 12, 0).wait_send()


def per_device(direction, plant, tile_pairs, mic_weight):
    device_id = lax.axis_index("spk")
    units, block, width = direction.shape
    tiles = plant.shape[0]
    bins = mic_weight.shape[0]
    group = SBLK // units
    per_a = MBLK // 8 // CHUNKS
    per_b = MBLK // 4 // CHUNKS
    rows_per = MBLK // group

    if bins == 1:
        weights = mic_weight.reshape(rows_per, block)
    else:
        whole = lax.all_gather(mic_weight, "spk", axis=1, tiled=True)
        weights = lax.dynamic_slice(
            whole, (device_id // group, (device_id % group) * rows_per, 0), (1, rows_per, block)
        )[0]

    bf16, f32 = jnp.bfloat16, jnp.float32
    dma = pltpu.SemaphoreType.DMA
    vmem = pl.BlockSpec(memory_space=pltpu.VMEM)
    hbm = pl.BlockSpec(memory_space=pl.ANY)
    smem = pl.BlockSpec(memory_space=pltpu.SMEM)
    piece = (CHUNKS, per_a, block, width)
    large = (CHUNKS, per_b, block, width)
    mixed = (CHUNKS, 2 * per_a + per_b, block, width)
    return pl.pallas_call(
        functools.partial(kernel, group),
        out_shape=jax.ShapeDtypeStruct(direction.shape, f32),
        in_specs=[smem, hbm, hbm, hbm],
        out_specs=vmem,
        scratch_shapes=[
            pltpu.VMEM(direction.shape, f32),
            pltpu.VMEM(plant.shape, bf16),
            pltpu.VMEM(weights.shape, f32),
            pltpu.VMEM((group, rows_per, block), f32),
            pltpu.VMEM((group, 8, block), f32),
            pltpu.VMEM((8, MBLK), jnp.int32),
            pltpu.SMEM((8, MBLK), jnp.int32),
            pltpu.VMEM((tiles * units + 1, block, width), f32),
            pltpu.VMEM((tiles // 2, 2 * block, 2 * block), bf16),
            pltpu.VMEM((2 * block, units * width), bf16),
            pltpu.VMEM(mixed, bf16),
            pltpu.VMEM(mixed, bf16),
            pltpu.VMEM((CHUNKS, per_a + per_b, block, width), f32),
        ] + [pltpu.VMEM(piece, bf16)] * 6 + [pltpu.VMEM(large, bf16)] * 5 + [
            pltpu.VMEM((MBLK + 1, block, width), bf16),
            pltpu.VMEM((tiles // 2, 2 * block, units * width), bf16),
            dma((4,)), dma((group,)), dma((group,)), dma((group,)), dma((group,)), dma((13,)),
        ] + [dma((CHUNKS,))] * 9 + [dma((3,))],
        compiler_params=pltpu.CompilerParams(
            collective_id=0, has_side_effects=True, vmem_limit_bytes=60 * 1024 * 1024
        ),
        name="pressure_matching",
    )(tile_pairs.T, direction, plant, weights)


def solution(mesh):
    placed = (
        P(("band", "spk"), None, None),
        P(("band", "spk"), None, None, None),
        P(("band", "spk"), None),
        P("band", "spk", None),
    )
    return jax.shard_map(
        per_device,
        mesh=mesh,
        in_specs=placed,
        out_specs=P(("band", "spk"), None, None),
        check_vma=False,
    )
```

```python
import functools

import jax
import jax.numpy as jnp
from jax import lax
from jax.experimental import pallas as pl
from jax.experimental.pallas import tpu as pltpu
from jax.sharding import PartitionSpec as P

SBLK = 32
MBLK = 128
SPEAKERS = 4096
CHUNKS = 16
LAG = 2

reg_weight = 0.25

MESH = pl.DeviceIdType.MESH


def kernel(
    group, pairs, direction_in, plant_in, weights_in, out,
    direction, plant, weights, info, power, table, slots, products, flipped, fields, sib_out, sib_in, own,
    y_out, y_in, right_out, left_out, from_left, from_right,
    root_out, root_left, root_right, swap_out, swap_in, weighted, stacked,
    load_s, info_s, info_r, power_s, power_r, sends,
    sib_r, y_r, right_r, left_r, wy_r, toward_right_r, toward_left_r, swap_r, spread_r, ends_r,
):
    units, block, width = direction.shape
    tiles = plant.shape[0]
    column = MBLK // 8
    square = MBLK // 4
    per_a = column // CHUNKS
    per_b = square // CHUNKS
    rows_per = MBLK // group
    depth = group // 4
    reach = depth // 2
    half = width // 2

    me = lax.axis_index("spk")
    base = (me // group) * group
    rank = me - base
    z = rank // 4
    y = (rank // 2) % 2
    c = rank % 2
    sib = me + 1 - 2 * c
    other_y = me + 2 - 4 * y
    q_mine = y * 2 + c
    q_sib = y * 2 + 1 - c
    q_y = (1 - y) * 2 + c
    q_diag = (1 - y) * 2 + 1 - c
    wide_mine = MBLK // 2 + c * square
    wide_sib = MBLK // 2 + (1 - c) * square
    has_left = z > 0
    has_right = z < depth - 1

    def peer(j):
        return base + (rank + j) % group

    def copy(src, dst, send, recv, device):
        return pltpu.make_async_remote_copy(
            src_ref=src, dst_ref=dst, send_sem=send, recv_sem=recv,
            device_id={"spk": device}, device_id_type=MESH,
        )

    early = tiles // 4
    loads = [
        pltpu.make_async_copy(src, dst, load_s.at[n])
        for n, (src, dst) in enumerate(
            [
                (direction_in, direction),
                (plant_in.at[pl.ds(0, early)], plant.at[pl.ds(0, early)]),
                (plant_in.at[pl.ds(early, tiles - early)], plant.at[pl.ds(early, tiles - early)]),
                (weights_in, weights),
            ]
        )
    ]
    for load in loads:
        load.start()
    barrier = pltpu.get_barrier_semaphore()
    for j in range(1, group):
        pl.semaphore_signal(barrier, inc=1, device_id={"spk": peer(j)}, device_id_type=MESH)

    row_id = lax.broadcasted_iota(jnp.int32, (8, MBLK), 0)
    lane_id = lax.broadcasted_iota(jnp.int32, (8, MBLK), 1)
    found = jnp.full((8, MBLK), tiles * units, jnp.int32)
    for t in range(tiles):
        u = pairs[0, t] % units
        hit = jnp.logical_and(row_id == u, lane_id == pairs[1, t])
        found = jnp.where(hit, t * units + u, found)
    table[...] = found
    to_slots = pltpu.make_async_copy(table, slots, load_s.at[4])
    to_slots.start()

    loads[0].wait()
    lane = lax.broadcasted_iota(jnp.int32, (block, width), 1)
    for u in range(units):
        x = direction[u]
        turned = pltpu.roll(x, half, 1)
        turned = jnp.where(lane < half, -turned, turned)
        fields[:block, u * width:(u + 1) * width] = x.astype(jnp.bfloat16)
        fields[block:, u * width:(u + 1) * width] = turned.astype(jnp.bfloat16)
    loads[1].wait()

    def multiply(t, carry):
        both = jnp.dot(
            jnp.concatenate([plant[t, 0], plant[t, 1]], axis=1),
            fields[...],
            preferred_element_type=jnp.float32,
        )
        for u in range(units):
            products[t * units + u] = both[:, u * width:(u + 1) * width]
        return carry

    lax.fori_loop(0, early, multiply, 0, unroll=2)
    loads[2].wait()
    lax.fori_loop(early, tiles, multiply, 0, unroll=4)
    products[tiles * units] = jnp.zeros((block, width), jnp.float32)
    weighted[MBLK] = jnp.zeros((block, width), jnp.bfloat16)
    loads[3].wait()
    info[rank] = weights[...]
    power[rank] = jnp.zeros((8, block), jnp.float32)
    to_slots.wait()

    pl.semaphore_wait(barrier, group - 1)

    def info_copy(j):
        return copy(info.at[rank], info.at[rank], info_s.at[j], info_r.at[j], peer(j))

    def part(q, k):
        return weighted.at[pl.ds(q * column + k * per_a, per_a)]

    def wide(first, k):
        return weighted.at[pl.ds(first + k * per_b, per_b)]

    def power_copy(j):
        return copy(power.at[rank], power.at[rank], power_s.at[j], power_r.at[j], peer(j))

    def sib_copy(k):
        return copy(sib_out.at[k], sib_in.at[k], sends.at[0], sib_r.at[k], sib)

    def y_copy(k):
        return copy(y_out.at[k], y_in.at[k], sends.at[1], y_r.at[k], other_y)

    def right_copy(k):
        return copy(right_out.at[k], from_left.at[k], sends.at[2], right_r.at[k], me + 4)

    def left_copy(k):
        return copy(left_out.at[k], from_right.at[k], sends.at[3], left_r.at[k], me - 4)

    def wy_copy(k):
        return copy(part(q_mine, k), part(q_mine, k), sends.at[4], wy_r.at[k], other_y)

    def ws_copy(k):
        return copy(part(q_mine, k), part(q_mine, k), sends.at[5], ends_r.at[0], sib)

    def wf_copy(k):
        return copy(part(q_y, k), part(q_y, k), sends.at[6], ends_r.at[1], sib)

    def wide_copy(k):
        return copy(wide(wide_mine, k), wide(wide_mine, k), sends.at[7], ends_r.at[2], sib)

    def toward_right(k):
        return copy(root_out.at[k], root_left.at[k], sends.at[8], toward_right_r.at[k], me + 4)

    def toward_left(k):
        return copy(root_out.at[k], root_right.at[k], sends.at[9], toward_left_r.at[k], me - 4)

    def swap_copy(k):
        return copy(swap_out.at[k], swap_in.at[k], sends.at[10], swap_r.at[k], other_y)

    def spread_right(k):
        return copy(wide(wide_mine, k), wide(wide_mine, k), sends.at[11], spread_r.at[k], me + 4)

    def spread_left(k):
        return copy(wide(wide_mine, k), wide(wide_mine, k), sends.at[12], spread_r.at[k], me - 4)

    for j in range(1, group):
        info_copy(j).start()

    def product(v):
        total = products[slots[0, v]]
        for u in range(1, units):
            total += products[slots[u, v]]
        return total

    def inside(k):
        return jnp.logical_and(k >= 0, k < CHUNKS)

    def scaled(v, pressure):
        row = info[v // rows_per, pl.ds(v % rows_per, 1), :]
        scale = jnp.broadcast_to(row, (block, block)).T
        weighted[v] = (scale * pressure).astype(jnp.bfloat16)

    def root_of(k):
        return reach - 1 + k % 2

    first = 10

    def after(hops):
        return 1 + LAG * (hops - 1)

    def step(s, carry):
        @pl.when(inside(s))
        def _():
            k = s
            for i in range(per_a):
                at = k * per_a + i
                sib_out[k, i] = product(q_sib * column + at).astype(jnp.bfloat16)
                sib_out[k, per_a + i] = product(q_diag * column + at).astype(jnp.bfloat16)
            for i in range(per_b):
                at = k * per_b + i
                sib_out[k, 2 * per_a + i] = product(wide_sib + at).astype(jnp.bfloat16)
            sib_copy(k).start()

        k1 = s - after(1)

        @pl.when(inside(k1))
        def _():
            sib_copy(k1).wait_recv()
            for i in range(per_a):
                total = product(q_y * column + k1 * per_a + i)
                total += sib_in[k1, per_a + i].astype(jnp.float32)
                y_out[k1, i] = total.astype(jnp.bfloat16)
            y_copy(k1).start()
            for i in range(per_b):
                at = per_a + i
                total = product(wide_mine + k1 * per_b + i)
                own[k1, at] = total + sib_in[k1, per_a + at].astype(jnp.float32)
            for i in range(per_a):
                total = product(q_mine * column + k1 * per_a + i)
                own[k1, i] = total + sib_in[k1, i].astype(jnp.float32)

        for d in range(reach, 0, -1):
            kb = s - after(1 + reach - d)
            gap = z - root_of(kb)

            @pl.when(jnp.logical_and(inside(kb), gap == -d))
            def _():
                @pl.when(has_left)
                def _():
                    toward_right(kb).wait_recv()
                    for i in range(per_b):
                        total = own[kb, per_a + i] + root_left[kb, i].astype(jnp.float32)
                        root_out[kb, i] = total.astype(jnp.bfloat16)

                @pl.when(jnp.logical_not(has_left))
                def _():
                    for i in range(per_b):
                        root_out[kb, i] = own[kb, per_a + i].astype(jnp.bfloat16)

                toward_right(kb).start()

            @pl.when(jnp.logical_and(inside(kb), gap == d))
            def _():
                @pl.when(has_right)
                def _():
                    toward_left(kb).wait_recv()
                    for i in range(per_b):
                        total = own[kb, per_a + i] + root_right[kb, i].astype(jnp.float32)
                        root_out[kb, i] = total.astype(jnp.bfloat16)

                @pl.when(jnp.logical_not(has_right))
                def _():
                    for i in range(per_b):
                        root_out[kb, i] = own[kb, per_a + i].astype(jnp.bfloat16)

                toward_left(kb).start()

        k2 = s - after(2)

        @pl.when(inside(k2))
        def _():
            y_copy(k2).wait_recv()
            for i in range(per_a):
                own[k2, i] = own[k2, i] + y_in[k2, i].astype(jnp.float32)

        kr = s - after(2 + z)

        @pl.when(inside(kr))
        def _():
            @pl.when(has_left)
            def _():
                right_copy(kr).wait_recv()

            @pl.when(jnp.logical_and(has_left, has_right))
            def _():
                for i in range(per_a):
                    total = own[kr, i] + from_left[kr, i].astype(jnp.float32)
                    right_out[kr, i] = total.astype(jnp.bfloat16)

            @pl.when(jnp.logical_not(has_left))
            def _():
                for i in range(per_a):
                    right_out[kr, i] = own[kr, i].astype(jnp.bfloat16)

            @pl.when(has_right)
            def _():
                right_copy(kr).start()

        kl = s - after(2 + depth - 1 - z)

        @pl.when(inside(kl))
        def _():
            @pl.when(has_right)
            def _():
                left_copy(kl).wait_recv()

            @pl.when(jnp.logical_and(has_left, has_right))
            def _():
                for i in range(per_a):
                    total = own[kl, i] + from_right[kl, i].astype(jnp.float32)
                    left_out[kl, i] = total.astype(jnp.bfloat16)

            @pl.when(jnp.logical_not(has_right))
            def _():
                for i in range(per_a):
                    left_out[kl, i] = own[kl, i].astype(jnp.bfloat16)

            @pl.when(has_left)
            def _():
                left_copy(kl).start()

        kc = s - after(1 + reach)

        @pl.when(jnp.logical_and(inside(kc), z == root_of(kc)))
        def _():
            @pl.when(has_left)
            def _():
                toward_right(kc).wait_recv()
                for i in range(per_b):
                    at = per_a + i
                    own[kc, at] = own[kc, at] + root_left[kc, i].astype(jnp.float32)

            @pl.when(has_right)
            def _():
                toward_left(kc).wait_recv()
                for i in range(per_b):
                    at = per_a + i
                    own[kc, at] = own[kc, at] + root_right[kc, i].astype(jnp.float32)

            for i in range(per_b):
                swap_out[kc, i] = own[kc, per_a + i].astype(jnp.bfloat16)
            swap_copy(kc).start()

        @pl.when(s == after(2 + reach))
        def _():
            for j in range(1, group):
                info_copy(j).wait_recv()

        kw = s - after(2 + reach)

        @pl.when(jnp.logical_and(inside(kw), z == root_of(kw)))
        def _():
            swap_copy(kw).wait_recv()
            for i in range(per_b):
                total = own[kw, per_a + i] + swap_in[kw, i].astype(jnp.float32)
                scaled(wide_mine + kw * per_b + i, total)

            @pl.when(has_left)
            def _():
                spread_left(kw).start()

            @pl.when(has_right)
            def _():
                spread_right(kw).start()

            wide_copy(kw).start()

        for d in range(1, reach + 1):
            ko = s - after(2 + reach + d)
            gap = z - root_of(ko)

            @pl.when(jnp.logical_and(inside(ko), gap == -d))
            def _():
                spread_left(ko).wait_recv()

                @pl.when(has_left)
                def _():
                    spread_left(ko).start()

                wide_copy(ko).start()

            @pl.when(jnp.logical_and(inside(ko), gap == d))
            def _():
                spread_right(ko).wait_recv()

                @pl.when(has_right)
                def _():
                    spread_right(ko).start()

                wide_copy(ko).start()

        kt = s - after(2 + jnp.maximum(z, depth - 1 - z))

        @pl.when(inside(kt))
        def _():
            @pl.when(has_left)
            def _():
                for i in range(per_a):
                    own[kt, i] = own[kt, i] + from_left[kt, i].astype(jnp.float32)

            @pl.when(has_right)
            def _():
                for i in range(per_a):
                    own[kt, i] = own[kt, i] + from_right[kt, i].astype(jnp.float32)

            for i in range(per_a):
                scaled(q_mine * column + kt * per_a + i, own[kt, i])
            wy_copy(kt).start()
            ws_copy(kt).start()

        kd = kt - LAG

        @pl.when(inside(kd))
        def _():
            wy_copy(kd).wait_recv()
            wf_copy(kd).start()

        n = s - first

        @pl.when(jnp.logical_and(n >= 0, n < tiles // 2))
        def _():
            squares = power[rank]
            for m in range(2):
                p0 = plant[2 * n + m, 0]
                p1 = plant[2 * n + m, 1]
                flipped[n, :block, m * block:(m + 1) * block] = p0.T
                flipped[n, block:, m * block:(m + 1) * block] = p1.T
                f0 = p0.astype(jnp.float32)
                f1 = p1.astype(jnp.float32)
                both = f0 * f0 + f1 * f1
                squares += jnp.sum(both.reshape(block // 8, 8, block), axis=0)
            power[rank] = squares

        @pl.when(n == tiles // 2)
        def _():
            for j in range(1, group):
                power_copy(j).start()

        return carry

    steps = max(CHUNKS + after(max(depth + 2, 2 + 2 * reach)), first + tiles // 2 + 1)
    lax.fori_loop(0, steps, step, 0)

    def whole_part(q):
        return weighted.at[pl.ds(q * column, column)]

    def whole_wide(first, amount):
        return weighted.at[pl.ds(first, amount)]

    def all_of(src, send, recv):
        return copy(src, src, sends.at[send], ends_r.at[recv], sib)

    all_of(whole_part(q_sib), 5, 0).wait_recv()
    all_of(whole_part(q_diag), 6, 1).wait_recv()
    all_of(whole_wide(wide_sib, square), 7, 2).wait_recv()

    for t in range(tiles):
        unit = pairs[0, t] % units
        rows = slice((t % 2) * block, (t % 2 + 1) * block)
        for u in range(units):
            at = jnp.where(unit == u, pairs[1, t], MBLK)
            stacked[t // 2, rows, u * width:(u + 1) * width] = weighted[at]
    total = jnp.zeros((2 * block, units * width), jnp.float32)
    for n in range(tiles // 2):
        total += jnp.dot(flipped[n], stacked[n], preferred_element_type=jnp.float32)

    for j in range(1, group):
        power_copy(j).wait_recv()
    power_sum = jnp.sum(power[...], axis=0)
    power_sum = jnp.sum(jnp.sum(power_sum, axis=1, keepdims=True), axis=0, keepdims=True)
    coefficient = reg_weight * power_sum / SPEAKERS
    for u in range(units):
        straight = total[:block, u * width:(u + 1) * width]
        crossed = pltpu.roll(total[block:, u * width:(u + 1) * width], half, 1)
        crossed = jnp.where(lane < half, crossed, -crossed)
        out[u] = straight + crossed + coefficient * direction[u]

    for j in range(1, group):
        info_copy(j).wait_send()
        power_copy(j).wait_send()

    all_of(sib_out, 0, 0).wait_send()
    all_of(y_out, 1, 0).wait_send()
    all_of(whole_part(q_mine), 4, 0).wait_send()
    all_of(whole_part(q_mine), 5, 0).wait_send()
    all_of(whole_part(q_y), 6, 0).wait_send()
    all_of(whole_wide(wide_mine, square), 7, 0).wait_send()

    @pl.when(has_right)
    def _():
        all_of(right_out, 2, 0).wait_send()

    @pl.when(has_left)
    def _():
        all_of(left_out, 3, 0).wait_send()

    some = square // 2

    @pl.when(z < reach - 1)
    def _():
        all_of(whole_wide(wide_mine, square), 8, 0).wait_send()

    @pl.when(z == reach - 1)
    def _():
        all_of(whole_wide(wide_mine, some), 8, 0).wait_send()
        all_of(whole_wide(wide_mine, some), 10, 0).wait_send()
        all_of(whole_wide(wide_mine, some), 11, 0).wait_send()

    @pl.when(z > reach)
    def _():
        all_of(whole_wide(wide_mine, square), 9, 0).wait_send()

    @pl.when(z == reach)
    def _():
        all_of(whole_wide(wide_mine, some), 9, 0).wait_send()
        all_of(whole_wide(wide_mine, some), 10, 0).wait_send()
        all_of(whole_wide(wide_mine, some), 12, 0).wait_send()

    @pl.when(jnp.logical_and(z >= reach, has_right))
    def _():
        all_of(whole_wide(wide_mine, square), 11, 0).wait_send()

    @pl.when(jnp.logical_and(z < reach, has_left))
    def _():
        all_of(whole_wide(wide_mine, square), 12, 0).wait_send()


def per_device(direction, plant, tile_pairs, mic_weight):
    device_id = lax.axis_index("spk")
    units, block, width = direction.shape
    tiles = plant.shape[0]
    bins = mic_weight.shape[0]
    group = SBLK // units
    per_a = MBLK // 8 // CHUNKS
    per_b = MBLK // 4 // CHUNKS
    rows_per = MBLK // group

    if bins == 1:
        weights = mic_weight.reshape(rows_per, block)
    else:
        whole = lax.all_gather(mic_weight, "spk", axis=1, tiled=True)
        weights = lax.dynamic_slice(
            whole, (device_id // group, (device_id % group) * rows_per, 0), (1, rows_per, block)
        )[0]

    bf16, f32 = jnp.bfloat16, jnp.float32
    dma = pltpu.SemaphoreType.DMA
    vmem = pl.BlockSpec(memory_space=pltpu.VMEM)
    hbm = pl.BlockSpec(memory_space=pl.ANY)
    smem = pl.BlockSpec(memory_space=pltpu.SMEM)
    piece = (CHUNKS, per_a, block, width)
    large = (CHUNKS, per_b, block, width)
    mixed = (CHUNKS, 2 * per_a + per_b, block, width)
    return pl.pallas_call(
        functools.partial(kernel, group),
        out_shape=jax.ShapeDtypeStruct(direction.shape, f32),
        in_specs=[smem, hbm, hbm, hbm],
        out_specs=vmem,
        scratch_shapes=[
            pltpu.VMEM(direction.shape, f32),
            pltpu.VMEM(plant.shape, bf16),
            pltpu.VMEM(weights.shape, f32),
            pltpu.VMEM((group, rows_per, block), f32),
            pltpu.VMEM((group, 8, block), f32),
            pltpu.VMEM((8, MBLK), jnp.int32),
            pltpu.SMEM((8, MBLK), jnp.int32),
            pltpu.VMEM((tiles * units + 1, block, width), f32),
            pltpu.VMEM((tiles // 2, 2 * block, 2 * block), bf16),
            pltpu.VMEM((2 * block, units * width), bf16),
            pltpu.VMEM(mixed, bf16),
            pltpu.VMEM(mixed, bf16),
            pltpu.VMEM((CHUNKS, per_a + per_b, block, width), f32),
        ] + [pltpu.VMEM(piece, bf16)] * 6 + [pltpu.VMEM(large, bf16)] * 5 + [
            pltpu.VMEM((MBLK + 1, block, width), bf16),
            pltpu.VMEM((tiles // 2, 2 * block, units * width), bf16),
            dma((5,)), dma((group,)), dma((group,)), dma((group,)), dma((group,)), dma((13,)),
        ] + [dma((CHUNKS,))] * 9 + [dma((3,))],
        compiler_params=pltpu.CompilerParams(
            collective_id=0, has_side_effects=True, vmem_limit_bytes=60 * 1024 * 1024
        ),
        name="pressure_matching",
    )(tile_pairs.T, direction, plant, weights)


def solution(mesh):
    placed = (
        P(("band", "spk"), None, None),
        P(("band", "spk"), None, None, None),
        P(("band", "spk"), None),
        P("band", "spk", None),
    )
    return jax.shard_map(
        per_device,
        mesh=mesh,
        in_specs=placed,
        out_specs=P(("band", "spk"), None, None),
        check_vma=False,
    )
```

```python
import functools

import jax
import jax.numpy as jnp
from jax import lax
from jax.experimental import pallas as pl
from jax.experimental.pallas import tpu as pltpu
from jax.sharding import PartitionSpec as P

SBLK = 32
MBLK = 128
SPEAKERS = 4096
CHUNKS = 16
LAG = 3

reg_weight = 0.25

MESH = pl.DeviceIdType.MESH


def kernel(
    group, pairs, direction_in, plant_in, weights_in, out,
    direction, plant, weights, info, power, table, slots, products, flipped, fields, sib_out, sib_in, own,
    y_out, y_in, right_out, left_out, from_left, from_right,
    root_out, root_left, root_right, swap_out, swap_in, weighted, stacked,
    load_s, info_s, info_r, power_s, power_r, sends,
    sib_r, y_r, right_r, left_r, wy_r, toward_right_r, toward_left_r, swap_r, spread_r, ends_r,
):
    units, block, width = direction.shape
    tiles = plant.shape[0]
    column = MBLK // 8
    square = MBLK // 4
    per_a = column // CHUNKS
    per_b = square // CHUNKS
    rows_per = MBLK // group
    depth = group // 4
    reach = depth // 2
    half = width // 2

    me = lax.axis_index("spk")
    base = (me // group) * group
    rank = me - base
    z = rank // 4
    y = (rank // 2) % 2
    c = rank % 2
    sib = me + 1 - 2 * c
    other_y = me + 2 - 4 * y
    q_mine = y * 2 + c
    q_sib = y * 2 + 1 - c
    q_y = (1 - y) * 2 + c
    q_diag = (1 - y) * 2 + 1 - c
    wide_mine = MBLK // 2 + c * square
    wide_sib = MBLK // 2 + (1 - c) * square
    has_left = z > 0
    has_right = z < depth - 1

    def peer(j):
        return base + (rank + j) % group

    def copy(src, dst, send, recv, device):
        return pltpu.make_async_remote_copy(
            src_ref=src, dst_ref=dst, send_sem=send, recv_sem=recv,
            device_id={"spk": device}, device_id_type=MESH,
        )

    early = tiles // 4
    loads = [
        pltpu.make_async_copy(src, dst, load_s.at[n])
        for n, (src, dst) in enumerate(
            [
                (direction_in, direction),
                (plant_in.at[pl.ds(0, early)], plant.at[pl.ds(0, early)]),
                (plant_in.at[pl.ds(early, tiles - early)], plant.at[pl.ds(early, tiles - early)]),
                (weights_in, weights),
            ]
        )
    ]
    for load in loads:
        load.start()
    barrier = pltpu.get_barrier_semaphore()
    for j in range(1, group):
        pl.semaphore_signal(barrier, inc=1, device_id={"spk": peer(j)}, device_id_type=MESH)

    row_id = lax.broadcasted_iota(jnp.int32, (8, MBLK), 0)
    lane_id = lax.broadcasted_iota(jnp.int32, (8, MBLK), 1)
    found = jnp.full((8, MBLK), tiles * units, jnp.int32)
    for t in range(tiles):
        u = pairs[0, t] % units
        hit = jnp.logical_and(row_id == u, lane_id == pairs[1, t])
        found = jnp.where(hit, t * units + u, found)
    table[...] = found
    to_slots = pltpu.make_async_copy(table, slots, load_s.at[4])
    to_slots.start()

    loads[0].wait()
    lane = lax.broadcasted_iota(jnp.int32, (block, width), 1)
    for u in range(units):
        x = direction[u]
        turned = pltpu.roll(x, half, 1)
        turned = jnp.where(lane < half, -turned, turned)
        fields[:block, u * width:(u + 1) * width] = x.astype(jnp.bfloat16)
        fields[block:, u * width:(u + 1) * width] = turned.astype(jnp.bfloat16)
    loads[1].wait()

    def multiply(t, carry):
        both = jnp.dot(
            jnp.concatenate([plant[t, 0], plant[t, 1]], axis=1),
            fields[...],
            preferred_element_type=jnp.float32,
        )
        for u in range(units):
            products[t * units + u] = both[:, u * width:(u + 1) * width]
        return carry

    lax.fori_loop(0, early, multiply, 0, unroll=2)
    loads[2].wait()
    lax.fori_loop(early, tiles, multiply, 0, unroll=4)
    products[tiles * units] = jnp.zeros((block, width), jnp.float32)
    weighted[MBLK] = jnp.zeros((block, width), jnp.bfloat16)
    loads[3].wait()
    info[rank] = weights[...]
    power[rank] = jnp.zeros((8, block), jnp.float32)
    to_slots.wait()

    pl.semaphore_wait(barrier, group - 1)

    def info_copy(j):
        return copy(info.at[rank], info.at[rank], info_s.at[j], info_r.at[j], peer(j))

    def part(q, k):
        return weighted.at[pl.ds(q * column + k * per_a, per_a)]

    def wide(first, k):
        return weighted.at[pl.ds(first + k * per_b, per_b)]

    def power_copy(j):
        return copy(power.at[rank], power.at[rank], power_s.at[j], power_r.at[j], peer(j))

    def sib_copy(k):
        return copy(sib_out.at[k], sib_in.at[k], sends.at[0], sib_r.at[k], sib)

    def y_copy(k):
        return copy(y_out.at[k], y_in.at[k], sends.at[1], y_r.at[k], other_y)

    def right_copy(k):
        return copy(right_out.at[k], from_left.at[k], sends.at[2], right_r.at[k], me + 4)

    def left_copy(k):
        return copy(left_out.at[k], from_right.at[k], sends.at[3], left_r.at[k], me - 4)

    def wy_copy(k):
        return copy(part(q_mine, k), part(q_mine, k), sends.at[4], wy_r.at[k], other_y)

    def ws_copy(k):
        return copy(part(q_mine, k), part(q_mine, k), sends.at[5], ends_r.at[0], sib)

    def wf_copy(k):
        return copy(part(q_y, k), part(q_y, k), sends.at[6], ends_r.at[1], sib)

    def wide_copy(k):
        return copy(wide(wide_mine, k), wide(wide_mine, k), sends.at[7], ends_r.at[2], sib)

    def toward_right(k):
        return copy(root_out.at[k], root_left.at[k], sends.at[8], toward_right_r.at[k], me + 4)

    def toward_left(k):
        return copy(root_out.at[k], root_right.at[k], sends.at[9], toward_left_r.at[k], me - 4)

    def swap_copy(k):
        return copy(swap_out.at[k], swap_in.at[k], sends.at[10], swap_r.at[k], other_y)

    def spread_right(k):
        return copy(wide(wide_mine, k), wide(wide_mine, k), sends.at[11], spread_r.at[k], me + 4)

    def spread_left(k):
        return copy(wide(wide_mine, k), wide(wide_mine, k), sends.at[12], spread_r.at[k], me - 4)

    for j in range(1, group):
        info_copy(j).start()

    def product(v):
        total = products[slots[0, v]]
        for u in range(1, units):
            total += products[slots[u, v]]
        return total

    def inside(k):
        return jnp.logical_and(k >= 0, k < CHUNKS)

    def scaled(v, pressure):
        row = info[v // rows_per, pl.ds(v % rows_per, 1), :]
        scale = jnp.broadcast_to(row, (block, block)).T
        weighted[v] = (scale * pressure).astype(jnp.bfloat16)

    def root_of(k):
        return reach - 1 + k % 2

    first = 12

    def after(hops):
        return 1 + LAG * (hops - 1)

    def step(s, carry):
        @pl.when(inside(s))
        def _():
            k = s
            for i in range(per_a):
                at = k * per_a + i
                sib_out[k, i] = product(q_sib * column + at).astype(jnp.bfloat16)
                sib_out[k, per_a + i] = product(q_diag * column + at).astype(jnp.bfloat16)
            for i in range(per_b):
                at = k * per_b + i
                sib_out[k, 2 * per_a + i] = product(wide_sib + at).astype(jnp.bfloat16)
            sib_copy(k).start()

        k1 = s - after(1)

        @pl.when(inside(k1))
        def _():
            sib_copy(k1).wait_recv()
            for i in range(per_a):
                total = product(q_y * column + k1 * per_a + i)
                total += sib_in[k1, per_a + i].astype(jnp.float32)
                y_out[k1, i] = total.astype(jnp.bfloat16)
            y_copy(k1).start()
            for i in range(per_b):
                at = per_a + i
                total = product(wide_mine + k1 * per_b + i)
                own[k1, at] = total + sib_in[k1, per_a + at].astype(jnp.float32)
            for i in range(per_a):
                total = product(q_mine * column + k1 * per_a + i)
                own[k1, i] = total + sib_in[k1, i].astype(jnp.float32)

        for d in range(reach, 0, -1):
            kb = s - after(1 + reach - d)
            gap = z - root_of(kb)

            @pl.when(jnp.logical_and(inside(kb), gap == -d))
            def _():
                @pl.when(has_left)
                def _():
                    toward_right(kb).wait_recv()
                    for i in range(per_b):
                        total = own[kb, per_a + i] + root_left[kb, i].astype(jnp.float32)
                        root_out[kb, i] = total.astype(jnp.bfloat16)

                @pl.when(jnp.logical_not(has_left))
                def _():
                    for i in range(per_b):
                        root_out[kb, i] = own[kb, per_a + i].astype(jnp.bfloat16)

                toward_right(kb).start()

            @pl.when(jnp.logical_and(inside(kb), gap == d))
            def _():
                @pl.when(has_right)
                def _():
                    toward_left(kb).wait_recv()
                    for i in range(per_b):
                        total = own[kb, per_a + i] + root_right[kb, i].astype(jnp.float32)
                        root_out[kb, i] = total.astype(jnp.bfloat16)

                @pl.when(jnp.logical_not(has_right))
                def _():
                    for i in range(per_b):
                        root_out[kb, i] = own[kb, per_a + i].astype(jnp.bfloat16)

                toward_left(kb).start()

        k2 = s - after(2)

        @pl.when(inside(k2))
        def _():
            y_copy(k2).wait_recv()
            for i in range(per_a):
                own[k2, i] = own[k2, i] + y_in[k2, i].astype(jnp.float32)

        kr = s - after(2 + z)

        @pl.when(inside(kr))
        def _():
            @pl.when(has_left)
            def _():
                right_copy(kr).wait_recv()

            @pl.when(jnp.logical_and(has_left, has_right))
            def _():
                for i in range(per_a):
                    total = own[kr, i] + from_left[kr, i].astype(jnp.float32)
                    right_out[kr, i] = total.astype(jnp.bfloat16)

            @pl.when(jnp.logical_not(has_left))
            def _():
                for i in range(per_a):
                    right_out[kr, i] = own[kr, i].astype(jnp.bfloat16)

            @pl.when(has_right)
            def _():
                right_copy(kr).start()

        kl = s - after(2 + depth - 1 - z)

        @pl.when(inside(kl))
        def _():
            @pl.when(has_right)
            def _():
                left_copy(kl).wait_recv()

            @pl.when(jnp.logical_and(has_left, has_right))
            def _():
                for i in range(per_a):
                    total = own[kl, i] + from_right[kl, i].astype(jnp.float32)
                    left_out[kl, i] = total.astype(jnp.bfloat16)

            @pl.when(jnp.logical_not(has_right))
            def _():
                for i in range(per_a):
                    left_out[kl, i] = own[kl, i].astype(jnp.bfloat16)

            @pl.when(has_left)
            def _():
                left_copy(kl).start()

        kc = s - after(1 + reach)

        @pl.when(jnp.logical_and(inside(kc), z == root_of(kc)))
        def _():
            @pl.when(has_left)
            def _():
                toward_right(kc).wait_recv()
                for i in range(per_b):
                    at = per_a + i
                    own[kc, at] = own[kc, at] + root_left[kc, i].astype(jnp.float32)

            @pl.when(has_right)
            def _():
                toward_left(kc).wait_recv()
                for i in range(per_b):
                    at = per_a + i
                    own[kc, at] = own[kc, at] + root_right[kc, i].astype(jnp.float32)

            for i in range(per_b):
                swap_out[kc, i] = own[kc, per_a + i].astype(jnp.bfloat16)
            swap_copy(kc).start()

        @pl.when(s == after(2 + reach))
        def _():
            for j in range(1, group):
                info_copy(j).wait_recv()

        kw = s - after(2 + reach)

        @pl.when(jnp.logical_and(inside(kw), z == root_of(kw)))
        def _():
            swap_copy(kw).wait_recv()
            for i in range(per_b):
                total = own[kw, per_a + i] + swap_in[kw, i].astype(jnp.float32)
                scaled(wide_mine + kw * per_b + i, total)

            @pl.when(has_left)
            def _():
                spread_left(kw).start()

            @pl.when(has_right)
            def _():
                spread_right(kw).start()

            wide_copy(kw).start()

        for d in range(1, reach + 1):
            ko = s - after(2 + reach + d)
            gap = z - root_of(ko)

            @pl.when(jnp.logical_and(inside(ko), gap == -d))
            def _():
                spread_left(ko).wait_recv()

                @pl.when(has_left)
                def _():
                    spread_left(ko).start()

                wide_copy(ko).start()

            @pl.when(jnp.logical_and(inside(ko), gap == d))
            def _():
                spread_right(ko).wait_recv()

                @pl.when(has_right)
                def _():
                    spread_right(ko).start()

                wide_copy(ko).start()

        kt = s - after(2 + jnp.maximum(z, depth - 1 - z))

        @pl.when(inside(kt))
        def _():
            @pl.when(has_left)
            def _():
                for i in range(per_a):
                    own[kt, i] = own[kt, i] + from_left[kt, i].astype(jnp.float32)

            @pl.when(has_right)
            def _():
                for i in range(per_a):
                    own[kt, i] = own[kt, i] + from_right[kt, i].astype(jnp.float32)

            for i in range(per_a):
                scaled(q_mine * column + kt * per_a + i, own[kt, i])
            wy_copy(kt).start()
            ws_copy(kt).start()

        kd = kt - LAG

        @pl.when(inside(kd))
        def _():
            wy_copy(kd).wait_recv()
            wf_copy(kd).start()

        n = s - first

        @pl.when(jnp.logical_and(n >= 0, n < tiles // 2))
        def _():
            squares = power[rank]
            for m in range(2):
                p0 = plant[2 * n + m, 0]
                p1 = plant[2 * n + m, 1]
                flipped[n, :block, m * block:(m + 1) * block] = p0.T
                flipped[n, block:, m * block:(m + 1) * block] = p1.T
                f0 = p0.astype(jnp.float32)
                f1 = p1.astype(jnp.float32)
                both = f0 * f0 + f1 * f1
                squares += jnp.sum(both.reshape(block // 8, 8, block), axis=0)
            power[rank] = squares

        @pl.when(n == tiles // 2)
        def _():
            for j in range(1, group):
                power_copy(j).start()

        return carry

    steps = max(CHUNKS + after(max(depth + 2, 2 + 2 * reach)), first + tiles // 2 + 1)
    lax.fori_loop(0, steps, step, 0)

    def whole_part(q):
        return weighted.at[pl.ds(q * column, column)]

    def whole_wide(first, amount):
        return weighted.at[pl.ds(first, amount)]

    def all_of(src, send, recv):
        return copy(src, src, sends.at[send], ends_r.at[recv], sib)

    all_of(whole_part(q_sib), 5, 0).wait_recv()
    all_of(whole_part(q_diag), 6, 1).wait_recv()
    all_of(whole_wide(wide_sib, square), 7, 2).wait_recv()

    for t in range(tiles):
        unit = pairs[0, t] % units
        rows = slice((t % 2) * block, (t % 2 + 1) * block)
        for u in range(units):
            at = jnp.where(unit == u, pairs[1, t], MBLK)
            stacked[t // 2, rows, u * width:(u + 1) * width] = weighted[at]
    total = jnp.zeros((2 * block, units * width), jnp.float32)
    for n in range(tiles // 2):
        total += jnp.dot(flipped[n], stacked[n], preferred_element_type=jnp.float32)

    for j in range(1, group):
        power_copy(j).wait_recv()
    power_sum = jnp.sum(power[...], axis=0)
    power_sum = jnp.sum(jnp.sum(power_sum, axis=1, keepdims=True), axis=0, keepdims=True)
    coefficient = reg_weight * power_sum / SPEAKERS
    for u in range(units):
        straight = total[:block, u * width:(u + 1) * width]
        crossed = pltpu.roll(total[block:, u * width:(u + 1) * width], half, 1)
        crossed = jnp.where(lane < half, crossed, -crossed)
        out[u] = straight + crossed + coefficient * direction[u]

    for j in range(1, group):
        info_copy(j).wait_send()
        power_copy(j).wait_send()

    all_of(sib_out, 0, 0).wait_send()
    all_of(y_out, 1, 0).wait_send()
    all_of(whole_part(q_mine), 4, 0).wait_send()
    all_of(whole_part(q_mine), 5, 0).wait_send()
    all_of(whole_part(q_y), 6, 0).wait_send()
    all_of(whole_wide(wide_mine, square), 7, 0).wait_send()

    @pl.when(has_right)
    def _():
        all_of(right_out, 2, 0).wait_send()

    @pl.when(has_left)
    def _():
        all_of(left_out, 3, 0).wait_send()

    some = square // 2

    @pl.when(z < reach - 1)
    def _():
        all_of(whole_wide(wide_mine, square), 8, 0).wait_send()

    @pl.when(z == reach - 1)
    def _():
        all_of(whole_wide(wide_mine, some), 8, 0).wait_send()
        all_of(whole_wide(wide_mine, some), 10, 0).wait_send()
        all_of(whole_wide(wide_mine, some), 11, 0).wait_send()

    @pl.when(z > reach)
    def _():
        all_of(whole_wide(wide_mine, square), 9, 0).wait_send()

    @pl.when(z == reach)
    def _():
        all_of(whole_wide(wide_mine, some), 9, 0).wait_send()
        all_of(whole_wide(wide_mine, some), 10, 0).wait_send()
        all_of(whole_wide(wide_mine, some), 12, 0).wait_send()

    @pl.when(jnp.logical_and(z >= reach, has_right))
    def _():
        all_of(whole_wide(wide_mine, square), 11, 0).wait_send()

    @pl.when(jnp.logical_and(z < reach, has_left))
    def _():
        all_of(whole_wide(wide_mine, square), 12, 0).wait_send()


def per_device(direction, plant, tile_pairs, mic_weight):
    device_id = lax.axis_index("spk")
    units, block, width = direction.shape
    tiles = plant.shape[0]
    bins = mic_weight.shape[0]
    group = SBLK // units
    per_a = MBLK // 8 // CHUNKS
    per_b = MBLK // 4 // CHUNKS
    rows_per = MBLK // group

    if bins == 1:
        weights = mic_weight.reshape(rows_per, block)
    else:
        whole = lax.all_gather(mic_weight, "spk", axis=1, tiled=True)
        weights = lax.dynamic_slice(
            whole, (device_id // group, (device_id % group) * rows_per, 0), (1, rows_per, block)
        )[0]

    bf16, f32 = jnp.bfloat16, jnp.float32
    dma = pltpu.SemaphoreType.DMA
    vmem = pl.BlockSpec(memory_space=pltpu.VMEM)
    hbm = pl.BlockSpec(memory_space=pl.ANY)
    smem = pl.BlockSpec(memory_space=pltpu.SMEM)
    piece = (CHUNKS, per_a, block, width)
    large = (CHUNKS, per_b, block, width)
    mixed = (CHUNKS, 2 * per_a + per_b, block, width)
    return pl.pallas_call(
        functools.partial(kernel, group),
        out_shape=jax.ShapeDtypeStruct(direction.shape, f32),
        in_specs=[smem, hbm, hbm, hbm],
        out_specs=vmem,
        scratch_shapes=[
            pltpu.VMEM(direction.shape, f32),
            pltpu.VMEM(plant.shape, bf16),
            pltpu.VMEM(weights.shape, f32),
            pltpu.VMEM((group, rows_per, block), f32),
            pltpu.VMEM((group, 8, block), f32),
            pltpu.VMEM((8, MBLK), jnp.int32),
            pltpu.SMEM((8, MBLK), jnp.int32),
            pltpu.VMEM((tiles * units + 1, block, width), f32),
            pltpu.VMEM((tiles // 2, 2 * block, 2 * block), bf16),
            pltpu.VMEM((2 * block, units * width), bf16),
            pltpu.VMEM(mixed, bf16),
            pltpu.VMEM(mixed, bf16),
            pltpu.VMEM((CHUNKS, per_a + per_b, block, width), f32),
        ] + [pltpu.VMEM(piece, bf16)] * 6 + [pltpu.VMEM(large, bf16)] * 5 + [
            pltpu.VMEM((MBLK + 1, block, width), bf16),
            pltpu.VMEM((tiles // 2, 2 * block, units * width), bf16),
            dma((5,)), dma((group,)), dma((group,)), dma((group,)), dma((group,)), dma((13,)),
        ] + [dma((CHUNKS,))] * 9 + [dma((3,))],
        compiler_params=pltpu.CompilerParams(
            collective_id=0, has_side_effects=True, vmem_limit_bytes=60 * 1024 * 1024
        ),
        name="pressure_matching",
    )(tile_pairs.T, direction, plant, weights)


def solution(mesh):
    placed = (
        P(("band", "spk"), None, None),
        P(("band", "spk"), None, None, None),
        P(("band", "spk"), None),
        P("band", "spk", None),
    )
    return jax.shard_map(
        per_device,
        mesh=mesh,
        in_specs=placed,
        out_specs=P(("band", "spk"), None, None),
        check_vma=False,
    )
```

```python
import functools

import jax
import jax.numpy as jnp
from jax import lax
from jax.experimental import pallas as pl
from jax.experimental.pallas import tpu as pltpu
from jax.sharding import PartitionSpec as P

SBLK = 32
MBLK = 128
SPEAKERS = 4096
CHUNKS = 16
LAG = 2

reg_weight = 0.25

MESH = pl.DeviceIdType.MESH


def kernel(
    group, pairs, direction_in, plant_in, weights_in, out,
    direction, plant, weights, info, power, table, slots, products, flipped, fields, sib_out, sib_in, own,
    y_out, y_in, right_out, left_out, from_left, from_right,
    root_out, root_left, root_right, swap_out, swap_in, weighted,
    load_s, info_s, info_r, power_s, power_r, sends,
    sib_r, y_r, right_r, left_r, wy_r, toward_right_r, toward_left_r, swap_r, spread_r, ends_r,
):
    units, block, width = direction.shape
    tiles = plant.shape[0]
    column = MBLK // 8
    square = MBLK // 4
    per_a = column // CHUNKS
    per_b = square // CHUNKS
    rows_per = MBLK // group
    depth = group // 4
    reach = depth // 2
    half = width // 2

    me = lax.axis_index("spk")
    base = (me // group) * group
    rank = me - base
    z = rank // 4
    y = (rank // 2) % 2
    c = rank % 2
    sib = me + 1 - 2 * c
    other_y = me + 2 - 4 * y
    q_mine = y * 2 + c
    q_sib = y * 2 + 1 - c
    q_y = (1 - y) * 2 + c
    q_diag = (1 - y) * 2 + 1 - c
    wide_mine = MBLK // 2 + c * square
    wide_sib = MBLK // 2 + (1 - c) * square
    has_left = z > 0
    has_right = z < depth - 1

    def peer(j):
        return base + (rank + j) % group

    def copy(src, dst, send, recv, device):
        return pltpu.make_async_remote_copy(
            src_ref=src, dst_ref=dst, send_sem=send, recv_sem=recv,
            device_id={"spk": device}, device_id_type=MESH,
        )

    early = tiles // 4
    loads = [
        pltpu.make_async_copy(src, dst, load_s.at[n])
        for n, (src, dst) in enumerate(
            [
                (direction_in, direction),
                (plant_in.at[pl.ds(0, early)], plant.at[pl.ds(0, early)]),
                (plant_in.at[pl.ds(early, tiles - early)], plant.at[pl.ds(early, tiles - early)]),
                (weights_in, weights),
            ]
        )
    ]
    for load in loads:
        load.start()
    barrier = pltpu.get_barrier_semaphore()
    for j in range(1, group):
        pl.semaphore_signal(barrier, inc=1, device_id={"spk": peer(j)}, device_id_type=MESH)

    row_id = lax.broadcasted_iota(jnp.int32, (8, MBLK), 0)
    lane_id = lax.broadcasted_iota(jnp.int32, (8, MBLK), 1)
    found = jnp.full((8, MBLK), tiles * units, jnp.int32)
    for t in range(tiles):
        u = pairs[0, t] % units
        hit = jnp.logical_and(row_id == u, lane_id == pairs[1, t])
        found = jnp.where(hit, t * units + u, found)
    table[...] = found
    to_slots = pltpu.make_async_copy(table, slots, load_s.at[4])
    to_slots.start()

    loads[0].wait()
    lane = lax.broadcasted_iota(jnp.int32, (block, width), 1)
    for u in range(units):
        x = direction[u]
        turned = pltpu.roll(x, half, 1)
        turned = jnp.where(lane < half, -turned, turned)
        fields[:block, u * width:(u + 1) * width] = x.astype(jnp.bfloat16)
        fields[block:, u * width:(u + 1) * width] = turned.astype(jnp.bfloat16)
    loads[1].wait()

    def multiply(t):
        both = jnp.dot(
            jnp.concatenate([plant[t, 0], plant[t, 1]], axis=1),
            fields[...],
            preferred_element_type=jnp.float32,
        )
        for u in range(units):
            products[t * units + u] = both[:, u * width:(u + 1) * width]

    for t in range(tiles):
        if t == early:
            loads[2].wait()
        multiply(t)
    products[tiles * units] = jnp.zeros((block, width), jnp.float32)
    weighted[MBLK] = jnp.zeros((block, width), jnp.bfloat16)
    loads[3].wait()
    info[rank] = weights[...]
    power[rank] = jnp.zeros((8, block), jnp.float32)
    to_slots.wait()

    pl.semaphore_wait(barrier, group - 1)

    def info_copy(j):
        return copy(info.at[rank], info.at[rank], info_s.at[j], info_r.at[j], peer(j))

    def part(q, k):
        return weighted.at[pl.ds(q * column + k * per_a, per_a)]

    def wide(first, k):
        return weighted.at[pl.ds(first + k * per_b, per_b)]

    def power_copy(j):
        return copy(power.at[rank], power.at[rank], power_s.at[j], power_r.at[j], peer(j))

    def sib_copy(k):
        return copy(sib_out.at[k], sib_in.at[k], sends.at[0], sib_r.at[k], sib)

    def y_copy(k):
        return copy(y_out.at[k], y_in.at[k], sends.at[1], y_r.at[k], other_y)

    def right_copy(k):
        return copy(right_out.at[k], from_left.at[k], sends.at[2], right_r.at[k], me + 4)

    def left_copy(k):
        return copy(left_out.at[k], from_right.at[k], sends.at[3], left_r.at[k], me - 4)

    def wy_copy(k):
        return copy(part(q_mine, k), part(q_mine, k), sends.at[4], wy_r.at[k], other_y)

    def ws_copy(k):
        return copy(part(q_mine, k), part(q_mine, k), sends.at[5], ends_r.at[0], sib)

    def wf_copy(k):
        return copy(part(q_y, k), part(q_y, k), sends.at[6], ends_r.at[1], sib)

    def wide_copy(k):
        return copy(wide(wide_mine, k), wide(wide_mine, k), sends.at[7], ends_r.at[2], sib)

    def toward_right(k):
        return copy(root_out.at[k], root_left.at[k], sends.at[8], toward_right_r.at[k], me + 4)

    def toward_left(k):
        return copy(root_out.at[k], root_right.at[k], sends.at[9], toward_left_r.at[k], me - 4)

    def swap_copy(k):
        return copy(swap_out.at[k], swap_in.at[k], sends.at[10], swap_r.at[k], other_y)

    def spread_right(k):
        return copy(wide(wide_mine, k), wide(wide_mine, k), sends.at[11], spread_r.at[k], me + 4)

    def spread_left(k):
        return copy(wide(wide_mine, k), wide(wide_mine, k), sends.at[12], spread_r.at[k], me - 4)

    for j in range(1, group):
        info_copy(j).start()

    def product(v):
        total = products[slots[0, v]]
        for u in range(1, units):
            total += products[slots[u, v]]
        return total

    def inside(k):
        return jnp.logical_and(k >= 0, k < CHUNKS)

    def scaled(v, pressure):
        row = info[v // rows_per, pl.ds(v % rows_per, 1), :]
        scale = jnp.broadcast_to(row, (block, block)).T
        weighted[v] = (scale * pressure).astype(jnp.bfloat16)

    def root_of(k):
        return reach - 1 + k % 2

    first = 10

    def after(hops):
        return 1 + LAG * (hops - 1)

    def step(s, carry):
        @pl.when(inside(s))
        def _():
            k = s
            for i in range(per_a):
                at = k * per_a + i
                sib_out[k, i] = product(q_sib * column + at).astype(jnp.bfloat16)
                sib_out[k, per_a + i] = product(q_diag * column + at).astype(jnp.bfloat16)
            for i in range(per_b):
                at = k * per_b + i
                sib_out[k, 2 * per_a + i] = product(wide_sib + at).astype(jnp.bfloat16)
            sib_copy(k).start()

        k1 = s - after(1)

        @pl.when(inside(k1))
        def _():
            sib_copy(k1).wait_recv()
            for i in range(per_a):
                total = product(q_y * column + k1 * per_a + i)
                total += sib_in[k1, per_a + i].astype(jnp.float32)
                y_out[k1, i] = total.astype(jnp.bfloat16)
            y_copy(k1).start()
            for i in range(per_b):
                at = per_a + i
                total = product(wide_mine + k1 * per_b + i)
                own[k1, at] = total + sib_in[k1, per_a + at].astype(jnp.float32)
            for i in range(per_a):
                total = product(q_mine * column + k1 * per_a + i)
                own[k1, i] = total + sib_in[k1, i].astype(jnp.float32)

        for d in range(reach, 0, -1):
            kb = s - after(1 + reach - d)
            gap = z - root_of(kb)

            @pl.when(jnp.logical_and(inside(kb), gap == -d))
            def _():
                @pl.when(has_left)
                def _():
                    toward_right(kb).wait_recv()
                    for i in range(per_b):
                        total = own[kb, per_a + i] + root_left[kb, i].astype(jnp.float32)
                        root_out[kb, i] = total.astype(jnp.bfloat16)

                @pl.when(jnp.logical_not(has_left))
                def _():
                    for i in range(per_b):
                        root_out[kb, i] = own[kb, per_a + i].astype(jnp.bfloat16)

                toward_right(kb).start()

            @pl.when(jnp.logical_and(inside(kb), gap == d))
            def _():
                @pl.when(has_right)
                def _():
                    toward_left(kb).wait_recv()
                    for i in range(per_b):
                        total = own[kb, per_a + i] + root_right[kb, i].astype(jnp.float32)
                        root_out[kb, i] = total.astype(jnp.bfloat16)

                @pl.when(jnp.logical_not(has_right))
                def _():
                    for i in range(per_b):
                        root_out[kb, i] = own[kb, per_a + i].astype(jnp.bfloat16)

                toward_left(kb).start()

        k2 = s - after(2)

        @pl.when(inside(k2))
        def _():
            y_copy(k2).wait_recv()
            for i in range(per_a):
                own[k2, i] = own[k2, i] + y_in[k2, i].astype(jnp.float32)

        kr = s - after(2 + z)

        @pl.when(inside(kr))
        def _():
            @pl.when(has_left)
            def _():
                right_copy(kr).wait_recv()

            @pl.when(jnp.logical_and(has_left, has_right))
            def _():
                for i in range(per_a):
                    total = own[kr, i] + from_left[kr, i].astype(jnp.float32)
                    right_out[kr, i] = total.astype(jnp.bfloat16)

            @pl.when(jnp.logical_not(has_left))
            def _():
                for i in range(per_a):
                    right_out[kr, i] = own[kr, i].astype(jnp.bfloat16)

            @pl.when(has_right)
            def _():
                right_copy(kr).start()

        kl = s - after(2 + depth - 1 - z)

        @pl.when(inside(kl))
        def _():
            @pl.when(has_right)
            def _():
                left_copy(kl).wait_recv()

            @pl.when(jnp.logical_and(has_left, has_right))
            def _():
                for i in range(per_a):
                    total = own[kl, i] + from_right[kl, i].astype(jnp.float32)
                    left_out[kl, i] = total.astype(jnp.bfloat16)

            @pl.when(jnp.logical_not(has_right))
            def _():
                for i in range(per_a):
                    left_out[kl, i] = own[kl, i].astype(jnp.bfloat16)

            @pl.when(has_left)
            def _():
                left_copy(kl).start()

        kc = s - after(1 + reach)

        @pl.when(jnp.logical_and(inside(kc), z == root_of(kc)))
        def _():
            @pl.when(has_left)
            def _():
                toward_right(kc).wait_recv()
                for i in range(per_b):
                    at = per_a + i
                    own[kc, at] = own[kc, at] + root_left[kc, i].astype(jnp.float32)

            @pl.when(has_right)
            def _():
                toward_left(kc).wait_recv()
                for i in range(per_b):
                    at = per_a + i
                    own[kc, at] = own[kc, at] + root_right[kc, i].astype(jnp.float32)

            for i in range(per_b):
                swap_out[kc, i] = own[kc, per_a + i].astype(jnp.bfloat16)
            swap_copy(kc).start()

        @pl.when(s == after(2 + reach))
        def _():
            for j in range(1, group):
                info_copy(j).wait_recv()

        kw = s - after(2 + reach)

        @pl.when(jnp.logical_and(inside(kw), z == root_of(kw)))
        def _():
            swap_copy(kw).wait_recv()
            for i in range(per_b):
                total = own[kw, per_a + i] + swap_in[kw, i].astype(jnp.float32)
                scaled(wide_mine + kw * per_b + i, total)

            @pl.when(has_left)
            def _():
                spread_left(kw).start()

            @pl.when(has_right)
            def _():
                spread_right(kw).start()

            wide_copy(kw).start()

        for d in range(1, reach + 1):
            ko = s - after(2 + reach + d)
            gap = z - root_of(ko)

            @pl.when(jnp.logical_and(inside(ko), gap == -d))
            def _():
                spread_left(ko).wait_recv()

                @pl.when(has_left)
                def _():
                    spread_left(ko).start()

                wide_copy(ko).start()

            @pl.when(jnp.logical_and(inside(ko), gap == d))
            def _():
                spread_right(ko).wait_recv()

                @pl.when(has_right)
                def _():
                    spread_right(ko).start()

                wide_copy(ko).start()

        kt = s - after(2 + jnp.maximum(z, depth - 1 - z))

        @pl.when(inside(kt))
        def _():
            @pl.when(has_left)
            def _():
                for i in range(per_a):
                    own[kt, i] = own[kt, i] + from_left[kt, i].astype(jnp.float32)

            @pl.when(has_right)
            def _():
                for i in range(per_a):
                    own[kt, i] = own[kt, i] + from_right[kt, i].astype(jnp.float32)

            for i in range(per_a):
                scaled(q_mine * column + kt * per_a + i, own[kt, i])
            wy_copy(kt).start()
            ws_copy(kt).start()

        kd = kt - LAG

        @pl.when(inside(kd))
        def _():
            wy_copy(kd).wait_recv()
            wf_copy(kd).start()

        n = s - first

        @pl.when(jnp.logical_and(n >= 0, n < tiles // 2))
        def _():
            squares = power[rank]
            for m in range(2):
                p0 = plant[2 * n + m, 0]
                p1 = plant[2 * n + m, 1]
                flipped[n, :block, m * block:(m + 1) * block] = p0.T
                flipped[n, block:, m * block:(m + 1) * block] = p1.T
                f0 = p0.astype(jnp.float32)
                f1 = p1.astype(jnp.float32)
                both = f0 * f0 + f1 * f1
                squares += jnp.sum(both.reshape(block // 8, 8, block), axis=0)
            power[rank] = squares

        @pl.when(n == tiles // 2)
        def _():
            for j in range(1, group):
                power_copy(j).start()

        return carry

    steps = max(CHUNKS + after(max(depth + 2, 2 + 2 * reach)), first + tiles // 2 + 1)
    lax.fori_loop(0, steps, step, 0)

    def whole_part(q):
        return weighted.at[pl.ds(q * column, column)]

    def whole_wide(first, amount):
        return weighted.at[pl.ds(first, amount)]

    def all_of(src, send, recv):
        return copy(src, src, sends.at[send], ends_r.at[recv], sib)

    all_of(whole_part(q_sib), 5, 0).wait_recv()
    all_of(whole_part(q_diag), 6, 1).wait_recv()
    all_of(whole_wide(wide_sib, square), 7, 2).wait_recv()

    def fields_of(t):
        unit = pairs[0, t] % units
        return jnp.concatenate(
            [weighted[jnp.where(unit == u, pairs[1, t], MBLK)] for u in range(units)], axis=1
        )

    total = jnp.zeros((2 * block, units * width), jnp.float32)
    for n in range(tiles // 2):
        stacked = jnp.concatenate([fields_of(2 * n), fields_of(2 * n + 1)], axis=0)
        total += jnp.dot(flipped[n], stacked, preferred_element_type=jnp.float32)

    for j in range(1, group):
        power_copy(j).wait_recv()
    power_sum = jnp.sum(power[...], axis=0)
    power_sum = jnp.sum(jnp.sum(power_sum, axis=1, keepdims=True), axis=0, keepdims=True)
    coefficient = reg_weight * power_sum / SPEAKERS
    for u in range(units):
        straight = total[:block, u * width:(u + 1) * width]
        crossed = pltpu.roll(total[block:, u * width:(u + 1) * width], half, 1)
        crossed = jnp.where(lane < half, crossed, -crossed)
        out[u] = straight + crossed + coefficient * direction[u]

    for j in range(1, group):
        info_copy(j).wait_send()
        power_copy(j).wait_send()

    all_of(sib_out, 0, 0).wait_send()
    all_of(y_out, 1, 0).wait_send()
    all_of(whole_part(q_mine), 4, 0).wait_send()
    all_of(whole_part(q_mine), 5, 0).wait_send()
    all_of(whole_part(q_y), 6, 0).wait_send()
    all_of(whole_wide(wide_mine, square), 7, 0).wait_send()

    @pl.when(has_right)
    def _():
        all_of(right_out, 2, 0).wait_send()

    @pl.when(has_left)
    def _():
        all_of(left_out, 3, 0).wait_send()

    some = square // 2

    @pl.when(z < reach - 1)
    def _():
        all_of(whole_wide(wide_mine, square), 8, 0).wait_send()

    @pl.when(z == reach - 1)
    def _():
        all_of(whole_wide(wide_mine, some), 8, 0).wait_send()
        all_of(whole_wide(wide_mine, some), 10, 0).wait_send()
        all_of(whole_wide(wide_mine, some), 11, 0).wait_send()

    @pl.when(z > reach)
    def _():
        all_of(whole_wide(wide_mine, square), 9, 0).wait_send()

    @pl.when(z == reach)
    def _():
        all_of(whole_wide(wide_mine, some), 9, 0).wait_send()
        all_of(whole_wide(wide_mine, some), 10, 0).wait_send()
        all_of(whole_wide(wide_mine, some), 12, 0).wait_send()

    @pl.when(jnp.logical_and(z >= reach, has_right))
    def _():
        all_of(whole_wide(wide_mine, square), 11, 0).wait_send()

    @pl.when(jnp.logical_and(z < reach, has_left))
    def _():
        all_of(whole_wide(wide_mine, square), 12, 0).wait_send()


def per_device(direction, plant, tile_pairs, mic_weight):
    device_id = lax.axis_index("spk")
    units, block, width = direction.shape
    tiles = plant.shape[0]
    bins = mic_weight.shape[0]
    group = SBLK // units
    per_a = MBLK // 8 // CHUNKS
    per_b = MBLK // 4 // CHUNKS
    rows_per = MBLK // group

    if bins == 1:
        weights = mic_weight.reshape(rows_per, block)
    else:
        whole = lax.all_gather(mic_weight, "spk", axis=1, tiled=True)
        weights = lax.dynamic_slice(
            whole, (device_id // group, (device_id % group) * rows_per, 0), (1, rows_per, block)
        )[0]

    bf16, f32 = jnp.bfloat16, jnp.float32
    dma = pltpu.SemaphoreType.DMA
    vmem = pl.BlockSpec(memory_space=pltpu.VMEM)
    hbm = pl.BlockSpec(memory_space=pl.ANY)
    smem = pl.BlockSpec(memory_space=pltpu.SMEM)
    piece = (CHUNKS, per_a, block, width)
    large = (CHUNKS, per_b, block, width)
    mixed = (CHUNKS, 2 * per_a + per_b, block, width)
    return pl.pallas_call(
        functools.partial(kernel, group),
        out_shape=jax.ShapeDtypeStruct(direction.shape, f32),
        in_specs=[smem, hbm, hbm, hbm],
        out_specs=vmem,
        scratch_shapes=[
            pltpu.VMEM(direction.shape, f32),
            pltpu.VMEM(plant.shape, bf16),
            pltpu.VMEM(weights.shape, f32),
            pltpu.VMEM((group, rows_per, block), f32),
            pltpu.VMEM((group, 8, block), f32),
            pltpu.VMEM((8, MBLK), jnp.int32),
            pltpu.SMEM((8, MBLK), jnp.int32),
            pltpu.VMEM((tiles * units + 1, block, width), f32),
            pltpu.VMEM((tiles // 2, 2 * block, 2 * block), bf16),
            pltpu.VMEM((2 * block, units * width), bf16),
            pltpu.VMEM(mixed, bf16),
            pltpu.VMEM(mixed, bf16),
            pltpu.VMEM((CHUNKS, per_a + per_b, block, width), f32),
        ] + [pltpu.VMEM(piece, bf16)] * 6 + [pltpu.VMEM(large, bf16)] * 5 + [
            pltpu.VMEM((MBLK + 1, block, width), bf16),
            dma((5,)), dma((group,)), dma((group,)), dma((group,)), dma((group,)), dma((13,)),
        ] + [dma((CHUNKS,))] * 9 + [dma((3,))],
        compiler_params=pltpu.CompilerParams(
            collective_id=0, has_side_effects=True, vmem_limit_bytes=60 * 1024 * 1024
        ),
        name="pressure_matching",
    )(tile_pairs.T, direction, plant, weights)


def solution(mesh):
    placed = (
        P(("band", "spk"), None, None),
        P(("band", "spk"), None, None, None),
        P(("band", "spk"), None),
        P("band", "spk", None),
    )
    return jax.shard_map(
        per_device,
        mesh=mesh,
        in_specs=placed,
        out_specs=P(("band", "spk"), None, None),
        check_vma=False,
    )
```
